32 devices in a mesh: ctx: 16 (over z, x, core), head: 2 (over y).
Axes of the slice: x: 2, y: 2, z: 4, core: 2. Of those that a mesh axis runs over, the one named last changes fastest.
Arguments:
- queries: bfloat16 [8192, 16, 128], P('ctx', 'head'), may hold values from -40 to 40
- keys: bfloat16 [8192, 128], P('ctx'), may hold values from -5 to 5
- values: bfloat16 [8192, 128], P('ctx'), may hold values from -1.5 to 1.5
- grad_out: bfloat16 [8192, 16, 128], P('ctx', 'head'), may hold values from -6 to 6
- lengths: int32 [16], replicated, may hold values from 1 to 1024, 8192 in all
- tile_of: int32 [16], replicated, may hold values from 0 to 15, each once
Outputs:
- attended: bfloat16 [8192, 16, 128], P('ctx', 'head')
- grad_queries: bfloat16 [8192, 16, 128], P('ctx', 'head')
- grad_keys: float32 [8192, 128], P('ctx')
- grad_values: float32 [8192, 128], P('ctx')
The draws below stay inside these ranges and needn't reach their ends.
Inputs may be any that keep to these rules, and one draw needn't show every extreme that they name: 16 positive lengths summing to 8192; the longest is exactly 1024. `tile_of`: each tile number appears once.
All inputs are finite; a program needn't handle non-finite values.
Results may differ from the reference program's by a relative error of at most 0.025.
Values may be sent and summed in bfloat16 or wider, within the bound.
No kernel may reach another device: no remote copies, remote signals or barrier semaphores. Data moves between devices by JAX's collectives and lax.ppermute only.
A program may use at most 128 MiB of HBM per device.

```python
import math
import jax
import jax.numpy as jnp
import numpy as np
from jax import lax

DH = 128
HQ = 16
TOK_DEV = 512
NDOCS = 16
TOKENS = 8192
MOST_DOC = 1024
N_CTX = 16


def draw_keys(key, part):
    result = jnp.clip(jax.random.normal(jax.random.fold_in(key, 13), (TOKENS, DH), jnp.float32), -4.0, 4.0)
    return result.astype(jnp.bfloat16)


def draw_queries(key, part):
    result = jnp.clip(jax.random.normal(jax.random.fold_in(key, 15), (TOKENS, HQ, DH), jnp.float32), -4.0, 4.0)
    return result.astype(jnp.bfloat16)


def steps_of(own_key, shape, pieces, smallest, top_value):
    def one(dim, blocks):
        heights = jax.random.uniform(jax.random.fold_in(jax.random.fold_in(own_key, 6), dim), (blocks,), jnp.float32, smallest / len(pieces), top_value / len(pieces))
        return jnp.repeat(jnp.exp(heights), shape[dim] // blocks).reshape((-1,) + (1,) * (len(shape) - dim - 1))

    level = one(*pieces[0])
    for cut in pieces[1:]:
        level = level * one(*cut)
    return level


def profile(amount, total, limit, lean):
    portions = [(1 << 20) // math.isqrt(rank ** lean) + 1 for rank in range(2, amount + 1)]
    spare, holding = total - limit - (amount - 1), [1] * (amount - 1)
    while spare > 0:
        movable = [i for i in range(amount - 1) if holding[i] < limit]
        mass, remaining = sum([portions[i] for i in movable]), spare
        for i in movable:
            addition = min(limit - holding[i], max(1, remaining * portions[i] // mass), spare)
            holding[i] = holding[i] + addition
            spare = spare - addition
    return np.array([limit] + holding)


def ragged(rng, number_of, total, reach, skew):
    if number_of == 2:
        one = jax.random.randint(rng, (), max(1, total - reach), min(reach, total - 1) + 1)
        return jnp.stack([one, total - one])
    sizes = jnp.asarray(profile(number_of, total, reach, skew), jnp.int32)
    couples = (number_of - 1) // 2
    source_of, taker = sizes[1:1 + 2 * couples:2], sizes[2:2 + 2 * couples:2]
    room = jnp.minimum(source_of - 1, reach - taker)
    shifted = jax.random.randint(jax.random.fold_in(rng, 1), (couples,), 0, 1 << 20) % (room + 1)
    sizes = sizes.at[1:1 + 2 * couples:2].set(source_of - shifted).at[2:2 + 2 * couples:2].set(taker + shifted)
    return sizes[jax.random.permutation(jax.random.fold_in(rng, 2), number_of)]


def bell_draw(stream_key, extent, deviation, reach, shards=(), held_as=jnp.bfloat16):
    factor_of = steps_of(stream_key, extent, shards, -0.22, 0.18) if shards else 1.0
    drawn = jax.random.normal(stream_key, extent, jnp.float32) * deviation * factor_of
    return jnp.minimum(jnp.maximum(drawn, -reach), reach).astype(held_as)


def setup_inputs(seed: int = 0) -> dict:
    arg_keys = jax.random.split(jax.random.key(seed), 7)
    queries = draw_queries(jax.random.fold_in(arg_keys[6], 71), 0)
    keys = draw_keys(jax.random.fold_in(arg_keys[6], 71), 0)
    values = bell_draw(arg_keys[2], (TOKENS, DH), 0.25, 1.5, ((0, 16),))
    grad_out = bell_draw(arg_keys[3], (TOKENS, HQ, DH), 1.0, 6.0, ((0, 16), (1, 2)))
    lengths = ragged(arg_keys[4], NDOCS, TOKENS, MOST_DOC, 2).astype(jnp.int32)
    tile_of = jax.random.permutation(arg_keys[5], N_CTX).astype(jnp.int32)
    return {"queries": queries, "keys": keys, "values": values, "grad_out": grad_out, "lengths": lengths, "tile_of": tile_of}


NEG_FILL = -1.0e30


def live_test(query_pos, query_doc, key_pos, key_doc):
    return (query_doc[:, None] == key_doc[None, :]) & (key_pos[None, :] <= query_pos[:, None])


def softmax_totals(query_rows, query_pos, query_doc, all_keys, key_pos, key_doc, key_block, score_scale):
    row_total = query_rows.shape[0]

    def loop_step(loop_index, carried):
        begin_row = (loop_index * key_block).astype(jnp.int32)
        key_rows = lax.dynamic_slice_in_dim(all_keys, begin_row, key_block, 0)
        block_pos = lax.dynamic_slice_in_dim(key_pos, begin_row, key_block, 0)
        block_doc = lax.dynamic_slice_in_dim(key_doc, begin_row, key_block, 0)
        live_mask = live_test(query_pos, query_doc, block_pos, block_doc)

        def update(state):
            running_max, running_sum = state
            scores = jnp.dot(query_rows, key_rows.T, preferred_element_type=jnp.float32) * score_scale
            scores = jnp.where(live_mask, scores, NEG_FILL)
            new_max = jnp.maximum(running_max, jnp.max(scores, axis=1))
            weights = jnp.where(live_mask, jnp.exp(scores - new_max[:, None]), 0.0)
            return new_max, running_sum * jnp.exp(running_max - new_max) + jnp.sum(weights, axis=1)

        return lax.cond(jnp.any(live_mask), update, lambda unchanged: unchanged, carried)

    start_state = (jnp.full((row_total,), NEG_FILL, jnp.float32), jnp.zeros((row_total,), jnp.float32))
    running_max, running_sum = lax.fori_loop(0, all_keys.shape[0] // key_block, loop_step, start_state)
    return running_max + jnp.log(running_sum)


def block_probs(query_rows, query_pos, query_doc, key_rows, block_pos, block_doc, log_total, score_scale):
    live_mask = live_test(query_pos, query_doc, block_pos, block_doc)
    scores = jnp.dot(query_rows, key_rows.T, preferred_element_type=jnp.float32) * score_scale
    return jnp.where(live_mask, jnp.exp(scores - log_total[:, None]), 0.0)


def attend_rows(query_rows, query_pos, query_doc, all_keys, all_values, key_pos, key_doc, key_block, log_total, score_scale):
    def loop_step(loop_index, accum):
        begin_row = (loop_index * key_block).astype(jnp.int32)
        key_rows = lax.dynamic_slice_in_dim(all_keys, begin_row, key_block, 0)
        value_rows = lax.dynamic_slice_in_dim(all_values, begin_row, key_block, 0)
        block_pos = lax.dynamic_slice_in_dim(key_pos, begin_row, key_block, 0)
        block_doc = lax.dynamic_slice_in_dim(key_doc, begin_row, key_block, 0)

        def update(total):
            probs = block_probs(query_rows, query_pos, query_doc, key_rows, block_pos, block_doc, log_total, score_scale)
            return total + jnp.dot(probs.astype(jnp.bfloat16), value_rows, preferred_element_type=jnp.float32)

        alive = jnp.any(live_test(query_pos, query_doc, block_pos, block_doc))
        return lax.cond(alive, update, lambda unchanged: unchanged, accum)

    start_total = jnp.zeros((query_rows.shape[0], all_values.shape[1]), jnp.float32)
    return lax.fori_loop(0, all_keys.shape[0] // key_block, loop_step, start_total)


def reference(queries, keys, values, grad_out, lengths, tile_of):
    score_scale = float(DH) ** -0.5
    offsets = jnp.arange(TOK_DEV, dtype=jnp.int32)
    positions = (tile_of[:, None].astype(jnp.int32) * TOK_DEV + offsets[None, :]).reshape(-1).astype(jnp.int32)
    doc_ends = jnp.cumsum(lengths).astype(jnp.int32)
    documents = jnp.sum((positions[:, None] >= doc_ends[None, :]).astype(jnp.int32), axis=1).astype(jnp.int32)
    key_block = TOK_DEV
    row_total = TOK_DEV * HQ

    def tile_step(grad_total, tile_index):
        begin_tile = (tile_index * TOK_DEV).astype(jnp.int32)
        query_rows = lax.dynamic_slice_in_dim(queries, begin_tile, TOK_DEV, 0).reshape(row_total, DH)
        cotangent_rows = lax.dynamic_slice_in_dim(grad_out, begin_tile, TOK_DEV, 0).reshape(row_total, DH)
        query_pos = jnp.repeat(lax.dynamic_slice_in_dim(positions, begin_tile, TOK_DEV, 0), HQ, total_repeat_length=row_total)
        query_doc = jnp.repeat(lax.dynamic_slice_in_dim(documents, begin_tile, TOK_DEV, 0), HQ, total_repeat_length=row_total)
        log_total = softmax_totals(query_rows, query_pos, query_doc, keys, positions, documents, key_block, score_scale)
        attended = attend_rows(query_rows, query_pos, query_doc, keys, values, positions, documents, key_block, log_total, score_scale).astype(jnp.bfloat16)
        row_delta = jnp.sum(cotangent_rows.astype(jnp.float32) * attended.astype(jnp.float32), axis=1)

        def loop_step(loop_index, carried):
            query_grad, grads = carried
            begin_row = (loop_index * key_block).astype(jnp.int32)
            key_rows = lax.dynamic_slice_in_dim(keys, begin_row, key_block, 0)
            value_rows = lax.dynamic_slice_in_dim(values, begin_row, key_block, 0)
            block_pos = lax.dynamic_slice_in_dim(positions, begin_row, key_block, 0)
            block_doc = lax.dynamic_slice_in_dim(documents, begin_row, key_block, 0)

            def update(state):
                query_grad, grads = state
                probs = block_probs(query_rows, query_pos, query_doc, key_rows, block_pos, block_doc, log_total, score_scale)
                probs_low = probs.astype(jnp.bfloat16)
                dprob = jnp.dot(cotangent_rows, value_rows.T, preferred_element_type=jnp.float32)
                dscore = (probs * (dprob - row_delta[:, None]) * score_scale).astype(jnp.bfloat16)
                query_grad = query_grad + jnp.dot(dscore, key_rows, preferred_element_type=jnp.float32)
                key_part = jnp.dot(dscore.T, query_rows, preferred_element_type=jnp.float32)
                value_part = jnp.dot(probs_low.T, cotangent_rows, preferred_element_type=jnp.float32)
                old_rows = lax.dynamic_slice_in_dim(grads, begin_row, key_block, 0)
                new_rows = old_rows + jnp.concatenate([key_part, value_part], axis=1)
                grads = lax.dynamic_update_slice(grads, new_rows, (begin_row, jnp.array(0, jnp.int32)))
                return query_grad, grads

            alive = jnp.any(live_test(query_pos, query_doc, block_pos, block_doc))
            return lax.cond(alive, update, lambda unchanged: unchanged, carried)

        start_state = (jnp.zeros((row_total, DH), jnp.float32), grad_total)
        query_grad, grad_total = lax.fori_loop(0, N_CTX, loop_step, start_state)
        return grad_total, (attended, query_grad.astype(jnp.bfloat16))

    grad_start = jnp.zeros((TOKENS, 2 * DH), jnp.float32)
    grad_total, (attended_tiles, query_tiles) = lax.scan(tile_step, grad_start, jnp.arange(N_CTX, dtype=jnp.int32))
    attended = attended_tiles.reshape(TOKENS, HQ, DH)
    grad_queries = query_tiles.reshape(TOKENS, HQ, DH)
    return attended, grad_queries, grad_total[:, :DH], grad_total[:, DH:]
```

```python
import functools

import jax
import jax.numpy as jnp
from jax import lax
from jax.experimental import pallas as pl
from jax.experimental.pallas import tpu as pltpu
from jax.sharding import PartitionSpec as P

LOG2E = 1.4426950408889634
NEG_FILL = -1e30
KEY_BLOCK = 256
ROW_BLOCK = 512
VMEM_LIMIT = 48 * 1024 * 1024


def matmul(left, right):
    return lax.dot_general(
        left, right, (((1,), (0,)), ((), ())), preferred_element_type=jnp.float32
    )


def fold_rows(block, combine):
    folded = block[0:8]
    for begin in range(8, block.shape[0], 8):
        folded = combine(folded, block[begin : begin + 8])
    return folded


def attention_kernel(
    window,
    heads,
    place_ref,
    lengths_ref,
    tile_of_ref,
    q_ref,
    g_ref,
    k_ref,
    v_ref,
    past_ref,
    att_ref,
    dq_ref,
    dkv_ref,
    k_win,
    v_win,
    k_turned,
    v_turned,
    score_buf,
    dk_acc,
    dv_acc,
):
    tile_rows, width = k_ref.shape
    scale = float(width) ** (-0.5)
    exponent_scale = scale * LOG2E
    my_tile = tile_of_ref[place_ref[0]]
    base = (my_tile - window) * tile_rows
    past_rows = window * tile_rows
    chunk_pos = ROW_BLOCK // heads
    ends = []
    total = jnp.int32(0)
    for doc in range(lengths_ref.shape[0]):
        total = total + lengths_ref[doc]
        ends.append(total)

    for slot in range(window):
        rows = pl.ds(slot * tile_rows, tile_rows)
        k_win[rows, :] = past_ref[0, slot]
        v_win[rows, :] = past_ref[1, slot]
    k_win[pl.ds(past_rows, tile_rows), :] = k_ref[...]
    v_win[pl.ds(past_rows, tile_rows), :] = v_ref[...]
    k_turned[...] = k_win[...].T
    v_turned[...] = v_win[...].T
    dk_acc[...] = jnp.zeros_like(dk_acc)
    dv_acc[...] = jnp.zeros_like(dv_acc)

    def chunk_step(chunk, carry):
        rows = pl.ds(pl.multiple_of(chunk * ROW_BLOCK, ROW_BLOCK), ROW_BLOCK)
        first_pos = my_tile * tile_rows + chunk * chunk_pos
        q_rows = q_ref[rows, :]
        g_rows = g_ref[rows, :]
        q_turned = q_rows.T
        g_turned = g_rows.T
        lane = lax.broadcasted_iota(jnp.int32, (1, ROW_BLOCK), 1)
        q_pos = first_pos + lax.div(lane, heads)
        start = jnp.zeros((1, ROW_BLOCK), jnp.int32)
        first_start = jnp.int32(0)
        for end in ends:
            start = jnp.where(end <= q_pos, end, start)
            first_start = jnp.where(end <= first_pos, end, first_start)
        low = start - base
        high = q_pos - base
        first_block = lax.div(jnp.maximum(first_start - base, 0), KEY_BLOCK)
        last_block = lax.div(past_rows + (chunk + 1) * chunk_pos - 1, KEY_BLOCK) + 1

        def block_rows(block):
            return pl.ds(pl.multiple_of(block * KEY_BLOCK, KEY_BLOCK), KEY_BLOCK)

        def score_step(block, top):
            keys = block_rows(block)
            score = matmul(k_win[keys, :], q_turned)
            key_pos = block * KEY_BLOCK + lax.broadcasted_iota(
                jnp.int32, (KEY_BLOCK, ROW_BLOCK), 0
            )
            score = jnp.where((key_pos >= low) & (key_pos <= high), score, NEG_FILL)
            score_buf[keys, :] = score
            return jnp.maximum(top, fold_rows(score, jnp.maximum))

        top = lax.fori_loop(
            first_block,
            last_block,
            score_step,
            jnp.full((8, ROW_BLOCK), NEG_FILL, jnp.float32),
        )
        top = jnp.max(top, axis=0, keepdims=True) * exponent_scale

        def weight_step(block, carried):
            sums, out_turned = carried
            keys = block_rows(block)
            weight = jnp.exp2(score_buf[keys, :] * exponent_scale - top)
            score_buf[keys, :] = weight
            out_turned = out_turned + matmul(v_turned[:, keys], weight.astype(jnp.bfloat16))
            return sums + fold_rows(weight, jnp.add), out_turned

        sums, out_turned = lax.fori_loop(
            first_block,
            last_block,
            weight_step,
            (
                jnp.zeros((8, ROW_BLOCK), jnp.float32),
                jnp.zeros((width, ROW_BLOCK), jnp.float32),
            ),
        )
        inverse = 1.0 / jnp.sum(sums, axis=0, keepdims=True)
        out_turned = out_turned * inverse
        att_ref[rows, :] = out_turned.T.astype(jnp.bfloat16)
        delta = jnp.sum(out_turned * g_turned.astype(jnp.float32), axis=0, keepdims=True)

        def grad_step(block, dq_turned):
            keys = block_rows(block)
            prob = score_buf[keys, :] * inverse
            dprob = matmul(v_win[keys, :], g_turned)
            dscore = (prob * (dprob - delta)).astype(jnp.bfloat16)
            dv_acc[keys, :] += matmul(prob.astype(jnp.bfloat16), g_rows)
            dk_acc[keys, :] += matmul(dscore, q_rows)
            return dq_turned + matmul(k_turned[:, keys], dscore)

        dq_turned = lax.fori_loop(
            first_block, last_block, grad_step, jnp.zeros((width, ROW_BLOCK), jnp.float32)
        )
        dq_ref[rows, :] = (dq_turned * scale).T.astype(jnp.bfloat16)
        return carry

    lax.fori_loop(0, q_ref.shape[0] // ROW_BLOCK, chunk_step, 0)
    dkv_ref[0] = (dk_acc[...] * scale).astype(jnp.bfloat16)
    dkv_ref[1] = dv_acc[...].astype(jnp.bfloat16)


def attention(window, heads, place, lengths, tile_of, q_rows, g_rows, keys, values, past):
    row_total, width = q_rows.shape
    tile_rows = keys.shape[0]
    span = (window + 1) * tile_rows
    smem = pl.BlockSpec(memory_space=pltpu.SMEM)
    vmem = pl.BlockSpec(memory_space=pltpu.VMEM)
    return pl.pallas_call(
        functools.partial(attention_kernel, window, heads),
        out_shape=(
            jax.ShapeDtypeStruct((row_total, width), jnp.bfloat16),
            jax.ShapeDtypeStruct((row_total, width), jnp.bfloat16),
            jax.ShapeDtypeStruct((2, span, width), jnp.bfloat16),
        ),
        in_specs=[smem] * 3 + [vmem] * 5,
        out_specs=(vmem,) * 3,
        scratch_shapes=[
            pltpu.VMEM((span, width), jnp.bfloat16),
            pltpu.VMEM((span, width), jnp.bfloat16),
            pltpu.VMEM((width, span), jnp.bfloat16),
            pltpu.VMEM((width, span), jnp.bfloat16),
            pltpu.VMEM((span, ROW_BLOCK), jnp.float32),
            pltpu.VMEM((span, width), jnp.float32),
            pltpu.VMEM((span, width), jnp.float32),
        ],
        compiler_params=pltpu.CompilerParams(vmem_limit_bytes=VMEM_LIMIT),
        name="attention",
    )(place, lengths, tile_of, q_rows, g_rows, keys, values, past)


def on_device(queries, keys, values, grad_out, lengths, tile_of):
    tile_rows, heads, width = queries.shape
    n_ctx = lax.axis_size("ctx")
    n_head = lax.axis_size("head")
    n_all = n_ctx * n_head
    piece = tile_rows // n_all
    both = ("ctx", "head")
    most_doc = n_ctx * tile_rows // 8
    window = -(-(most_doc - 1) // tile_rows)
    place = lax.axis_index("ctx").astype(jnp.int32).reshape(1)
    y = lax.axis_index("head")
    tiles = jnp.arange(n_ctx, dtype=jnp.int32)
    holder_hot = tile_of[None, :] == tiles[:, None]

    pieces = jnp.stack([keys, values]).reshape(2, n_ctx, n_head, piece, width)
    mine = lax.dynamic_index_in_dim(pieces, y, 2, keepdims=False)
    held = lax.all_to_all(mine.transpose(1, 0, 2, 3), "ctx", 0, 0, tiled=True)
    slots = window - jnp.arange(window, dtype=jnp.int32)
    wanted = tile_of[:, None] - slots[None, :]
    source_hot = (tile_of[None, None, :] == wanted[:, :, None]).astype(jnp.bfloat16)
    packed = jnp.einsum(
        "dsi,ie->dse",
        source_hot,
        held.reshape(n_ctx, 2 * piece * width),
        preferred_element_type=jnp.float32,
    ).astype(jnp.bfloat16)
    packed = jnp.broadcast_to(
        packed.reshape(n_ctx, 1, window, 2, piece, width),
        (n_ctx, n_head, window, 2, piece, width),
    ).reshape(n_all, window, 2, piece, width)
    past = lax.all_to_all(packed, both, 0, 0, tiled=True)
    past = past.transpose(2, 1, 0, 3, 4).reshape(2, window, tile_rows, width)

    attended, query_grad, grads = attention(
        window,
        heads,
        place,
        lengths,
        tile_of,
        queries.reshape(tile_rows * heads, width),
        grad_out.reshape(tile_rows * heads, width),
        keys,
        values,
        past,
    )

    grads = grads.reshape(2, window + 1, n_all, piece, width).transpose(2, 1, 0, 3, 4)
    terms = lax.all_to_all(grads, both, 0, 0, tiled=True)
    terms = terms.reshape(n_ctx, n_head, window + 1, 2 * piece * width)
    terms = jnp.sum(terms.astype(jnp.float32), axis=1)
    all_slots = window - jnp.arange(window + 1, dtype=jnp.int32)
    target = tile_of[:, None] - all_slots[None, :]
    summed = jnp.zeros((n_ctx, 2 * piece * width), jnp.float32)
    target_hot = (tile_of[:, None, None] == target[None, :, :]).astype(jnp.float32)
    summed = jnp.einsum(
        "ids,dse->ie", target_hot, terms, precision=lax.Precision.HIGHEST
    )
    summed = jnp.broadcast_to(
        summed.astype(jnp.bfloat16).reshape(n_ctx, 1, 2, piece, width),
        (n_ctx, n_head, 2, piece, width),
    ).reshape(n_all, 2, piece, width)
    result = lax.all_to_all(summed, both, 0, 0, tiled=True)
    result = result.transpose(1, 0, 2, 3).reshape(2, tile_rows, width).astype(jnp.float32)
    return (
        attended.reshape(tile_rows, heads, width),
        query_grad.reshape(tile_rows, heads, width),
        result[0],
        result[1],
    )


def solution(mesh):
    return jax.shard_map(
        on_device,
        mesh=mesh,
        in_specs=(
            P("ctx", "head", None),
            P("ctx", None),
            P("ctx", None),
            P("ctx", "head", None),
            P(),
            P(),
        ),
        out_specs=(P("ctx", "head", None), P("ctx", "head", None), P("ctx", None), P("ctx", None)),
        check_vma=False,
    )
```

```python
import functools

import jax
import jax.numpy as jnp
from jax import lax
from jax.experimental import pallas as pl
from jax.experimental.pallas import tpu as pltpu
from jax.sharding import PartitionSpec as P

LOG2E = 1.4426950408889634
NEG_FILL = -1e30
KEY_BLOCK = 256
ROW_BLOCK = 512
VMEM_LIMIT = 48 * 1024 * 1024
SMEM = pl.BlockSpec(memory_space=pltpu.SMEM)
F32 = jnp.float32
BF16 = jnp.bfloat16


def matmul(left, right):
    return lax.dot_general(left, right, (((1,), (0,)), ((), ())), preferred_element_type=F32)


def fold_rows(block, combine):
    folded = block[0:8]
    for begin in range(8, block.shape[0], 8):
        folded = combine(folded, block[begin : begin + 8])
    return folded


def block_rows(block):
    return pl.ds(pl.multiple_of(block * KEY_BLOCK, KEY_BLOCK), KEY_BLOCK)


class Spans:
    def __init__(self, heads, tile_rows, place_ref, lengths_ref, tile_of_ref, back):
        chunk = pl.program_id(0)
        chunk_pos = ROW_BLOCK // heads
        self.my_tile = tile_of_ref[place_ref[0]]
        self.base = (self.my_tile - back) * tile_rows
        self.first_pos = self.my_tile * tile_rows + chunk * chunk_pos
        self.ends = []
        total = jnp.int32(0)
        for doc in range(lengths_ref.shape[0]):
            total = total + lengths_ref[doc]
            self.ends.append(total)
        first_start = jnp.int32(0)
        for end in self.ends:
            first_start = jnp.where(end <= self.first_pos, end, first_start)
        self.first_block = lax.div(jnp.maximum(first_start - self.base, 0), KEY_BLOCK)
        reach = self.first_pos + chunk_pos - 1 - self.base
        self.last_block = lax.div(reach, KEY_BLOCK) + 1
        self.heads = heads

    def limits(self):
        lane = lax.broadcasted_iota(jnp.int32, (1, ROW_BLOCK), 1)
        q_pos = self.first_pos + lax.div(lane, self.heads)
        start = jnp.zeros((1, ROW_BLOCK), jnp.int32)
        for end in self.ends:
            start = jnp.where(end <= q_pos, end, start)
        return start - self.base, q_pos - self.base


def key_positions(block):
    return block * KEY_BLOCK + lax.broadcasted_iota(jnp.int32, (KEY_BLOCK, ROW_BLOCK), 0)


def own_forward_kernel(
    heads,
    place_ref,
    lengths_ref,
    tile_of_ref,
    q_ref,
    g_ref,
    k_ref,
    v_ref,
    q_turned_ref,
    g_turned_ref,
    weight_ref,
    out_ref,
    stats_ref,
    v_turned,
    score_buf,
):
    tile_rows, width = k_ref.shape
    exponent_scale = float(width) ** (-0.5) * LOG2E
    spans = Spans(heads, tile_rows, place_ref, lengths_ref, tile_of_ref, 0)

    @pl.when(pl.program_id(0) == 0)
    def turn_values():
        v_turned[...] = v_ref[...].T

    q_turned = q_ref[...].T
    q_turned_ref[...] = q_turned
    g_turned_ref[...] = g_ref[...].T
    low, high = spans.limits()

    def score_step(block, top):
        keys = block_rows(block)
        score = matmul(k_ref[keys, :], q_turned)
        key_pos = key_positions(block)
        score = jnp.where((key_pos >= low) & (key_pos <= high), score, NEG_FILL)
        score_buf[keys, :] = score
        return jnp.maximum(top, fold_rows(score, jnp.maximum))

    top = lax.fori_loop(
        spans.first_block,
        spans.last_block,
        score_step,
        jnp.full((8, ROW_BLOCK), NEG_FILL, F32),
    )
    top = jnp.max(top, axis=0, keepdims=True) * exponent_scale

    def weight_step(block, carried):
        sums, out_turned = carried
        keys = block_rows(block)
        weight = jnp.exp2(score_buf[keys, :] * exponent_scale - top)
        weight_low = weight.astype(BF16)
        weight_ref[keys, :] = weight_low
        out_turned = out_turned + matmul(v_turned[:, keys], weight_low)
        return sums + fold_rows(weight, jnp.add), out_turned

    sums, out_turned = lax.fori_loop(
        spans.first_block,
        spans.last_block,
        weight_step,
        (jnp.zeros((8, ROW_BLOCK), F32), jnp.zeros((width, ROW_BLOCK), F32)),
    )
    out_ref[...] = out_turned
    stats_ref[0:1, :] = top
    stats_ref[1:2, :] = jnp.sum(sums, axis=0, keepdims=True)


def unpack(window, tile_rows, pieces_ref, store):
    n_all, _, piece, _ = pieces_ref.shape
    for slot in range(window):
        for owner in range(n_all):
            begin = slot * tile_rows + owner * piece
            store(begin, piece, pieces_ref[owner, slot])


def pack(window, tile_rows, pieces_ref, load):
    n_all, _, piece, _ = pieces_ref.shape
    for slot in range(window):
        for owner in range(n_all):
            begin = slot * tile_rows + owner * piece
            pieces_ref[owner, slot] = load(begin, piece)


def past_weights_kernel(
    window,
    heads,
    tile_rows,
    place_ref,
    lengths_ref,
    tile_of_ref,
    q_turned_ref,
    g_ref,
    own_stats_ref,
    past_keys_ref,
    prob_ref,
    stats_ref,
    dv_ref,
    k_win,
    score_buf,
    dv_acc,
):
    width = k_win.shape[1]
    past_blocks = window * tile_rows // KEY_BLOCK
    exponent_scale = float(width) ** (-0.5) * LOG2E
    spans = Spans(heads, tile_rows, place_ref, lengths_ref, tile_of_ref, window)
    first_block = spans.first_block

    @pl.when(pl.program_id(0) == 0)
    def begin():
        def store(begin_row, size, rows):
            k_win[begin_row : begin_row + size, :] = rows

        unpack(window, tile_rows, past_keys_ref, store)
        dv_acc[...] = jnp.zeros_like(dv_acc)

    q_turned = q_turned_ref[...]
    g_rows = g_ref[...]
    low, _ = spans.limits()

    def score_step(block, top):
        keys = block_rows(block)
        score = matmul(k_win[keys, :], q_turned)
        score = jnp.where(key_positions(block) >= low, score, NEG_FILL)
        score_buf[keys, :] = score
        return jnp.maximum(top, fold_rows(score, jnp.maximum))

    past_top = lax.fori_loop(
        first_block, past_blocks, score_step, jnp.full((8, ROW_BLOCK), NEG_FILL, F32)
    )
    past_top = jnp.max(past_top, axis=0, keepdims=True) * exponent_scale
    own_top = own_stats_ref[0:1, :]
    top = jnp.maximum(own_top, past_top)

    def weight_step(block, sums):
        keys = block_rows(block)
        weight = jnp.exp2(score_buf[keys, :] * exponent_scale - top)
        score_buf[keys, :] = weight
        return sums + fold_rows(weight, jnp.add)

    sums = lax.fori_loop(
        first_block, past_blocks, weight_step, jnp.zeros((8, ROW_BLOCK), F32)
    )
    rescale = jnp.exp2(own_top - top)
    inverse = 1.0 / (
        own_stats_ref[1:2, :] * rescale + jnp.sum(sums, axis=0, keepdims=True)
    )
    stats_ref[0:1, :] = rescale * inverse

    def value_step(block, carry):
        keys = block_rows(block)
        prob = (score_buf[keys, :] * inverse).astype(BF16)
        prob_ref[keys, :] = prob
        dv_acc[keys, :] += matmul(prob, g_rows)
        return carry

    lax.fori_loop(first_block, past_blocks, value_step, 0)

    @pl.when(pl.program_id(0) == pl.num_programs(0) - 1)
    def finish():
        pack(
            window,
            tile_rows,
            dv_ref,
            lambda begin_row, size: dv_acc[begin_row : begin_row + size, :].astype(BF16),
        )


def past_grads_kernel(
    window,
    heads,
    tile_rows,
    place_ref,
    lengths_ref,
    tile_of_ref,
    q_ref,
    g_turned_ref,
    prob_ref,
    stats_ref,
    own_out_ref,
    past_keys_ref,
    past_values_ref,
    att_ref,
    delta_ref,
    dq_ref,
    dk_ref,
    k_win,
    v_win,
    k_turned,
    v_turned,
    dk_acc,
):
    width = k_win.shape[1]
    past_blocks = window * tile_rows // KEY_BLOCK
    scale = float(width) ** (-0.5)
    spans = Spans(heads, tile_rows, place_ref, lengths_ref, tile_of_ref, window)
    first_block = spans.first_block

    @pl.when(pl.program_id(0) == 0)
    def begin():
        def store_keys(begin_row, size, rows):
            k_win[begin_row : begin_row + size, :] = rows

        def store_values(begin_row, size, rows):
            v_win[begin_row : begin_row + size, :] = rows

        unpack(window, tile_rows, past_keys_ref, store_keys)
        unpack(window, tile_rows, past_values_ref, store_values)
        k_turned[...] = k_win[...].T
        v_turned[...] = v_win[...].T
        dk_acc[...] = jnp.zeros_like(dk_acc)

    q_rows = q_ref[...]
    g_turned = g_turned_ref[...]

    def attend_step(block, out_turned):
        keys = block_rows(block)
        return out_turned + matmul(v_turned[:, keys], prob_ref[keys, :])

    out_turned = lax.fori_loop(
        first_block, past_blocks, attend_step, own_out_ref[...] * stats_ref[0:1, :]
    )
    att_ref[...] = out_turned.T.astype(BF16)
    delta = jnp.sum(out_turned * g_turned.astype(F32), axis=0, keepdims=True)
    delta_ref[0:1, :] = delta

    def grad_step(block, dq_turned):
        keys = block_rows(block)
        dprob = matmul(v_win[keys, :], g_turned)
        dscore = (prob_ref[keys, :].astype(F32) * (dprob - delta)).astype(BF16)
        dk_acc[keys, :] += matmul(dscore, q_rows)
        return dq_turned + matmul(k_turned[:, keys], dscore)

    dq_ref[...] = lax.fori_loop(
        first_block, past_blocks, grad_step, jnp.zeros((width, ROW_BLOCK), F32)
    )

    @pl.when(pl.program_id(0) == pl.num_programs(0) - 1)
    def finish():
        pack(
            window,
            tile_rows,
            dk_ref,
            lambda begin_row, size: (
                dk_acc[begin_row : begin_row + size, :] * scale
            ).astype(BF16),
        )


def own_grads_kernel(
    heads,
    place_ref,
    lengths_ref,
    tile_of_ref,
    q_ref,
    g_ref,
    g_turned_ref,
    weight_ref,
    stats_ref,
    delta_ref,
    past_dq_ref,
    k_ref,
    v_ref,
    dq_ref,
    dkv_ref,
    k_turned,
    dk_acc,
    dv_acc,
):
    tile_rows, width = k_ref.shape
    scale = float(width) ** (-0.5)
    spans = Spans(heads, tile_rows, place_ref, lengths_ref, tile_of_ref, 0)

    @pl.when(pl.program_id(0) == 0)
    def begin():
        k_turned[...] = k_ref[...].T
        dk_acc[...] = jnp.zeros_like(dk_acc)
        dv_acc[...] = jnp.zeros_like(dv_acc)

    q_rows = q_ref[...]
    g_rows = g_ref[...]
    g_turned = g_turned_ref[...]
    rescale = stats_ref[0:1, :]
    delta = delta_ref[0:1, :]

    def grad_step(block, dq_turned):
        keys = block_rows(block)
        prob = weight_ref[keys, :].astype(F32) * rescale
        dprob = matmul(v_ref[keys, :], g_turned)
        dscore = (prob * (dprob - delta)).astype(BF16)
        dv_acc[keys, :] += matmul(prob.astype(BF16), g_rows)
        dk_acc[keys, :] += matmul(dscore, q_rows)
        return dq_turned + matmul(k_turned[:, keys], dscore)

    dq_turned = lax.fori_loop(
        spans.first_block, spans.last_block, grad_step, past_dq_ref[...]
    )
    dq_ref[...] = (dq_turned * scale).T.astype(BF16)

    @pl.when(pl.program_id(0) == pl.num_programs(0) - 1)
    def finish():
        dkv_ref[0] = (dk_acc[...] * scale).astype(BF16)
        dkv_ref[1] = dv_acc[...].astype(BF16)


def route_kernel(window, tile_of_ref, held_ref, out_ref, holder):
    n_ctx, n_head = out_ref.shape[:2]
    for ctx in range(n_ctx):
        holder[tile_of_ref[ctx]] = ctx

    def one(ctx, carry):
        for slot in range(window):
            tile = tile_of_ref[ctx] - (window - slot)
            source = holder[jnp.maximum(tile, 0)]
            rows = held_ref[source]
            for head in range(n_head):
                out_ref[ctx, head, slot] = rows
        return carry

    lax.fori_loop(0, n_ctx, one, 0)


def sum_kernel(window, tile_of_ref, terms_ref, out_ref, holder):
    n_ctx, n_head = out_ref.shape[:2]
    for ctx in range(n_ctx):
        holder[tile_of_ref[ctx]] = ctx

    def one(ctx, carry):
        total = jnp.zeros(out_ref.shape[2:], F32)
        for slot in range(window):
            tile = tile_of_ref[ctx] + (window - slot)
            source = holder[jnp.minimum(tile, n_ctx - 1)]
            part = terms_ref[source, 0, slot].astype(F32)
            for head in range(1, n_head):
                part = part + terms_ref[source, head, slot].astype(F32)
            total = total + jnp.where(tile < n_ctx, part, 0.0)
        for head in range(n_head):
            out_ref[ctx, head] = total.astype(BF16)
        return carry

    lax.fori_loop(0, n_ctx, one, 0)


def whole(shape):
    return pl.BlockSpec(shape, lambda chunk: (0,) * len(shape))


def rows_of(width):
    return pl.BlockSpec((ROW_BLOCK, width), lambda chunk: (chunk, 0))


def columns_of(height):
    return pl.BlockSpec((height, ROW_BLOCK), lambda chunk: (0, chunk))


def shape_of(shape, dtype):
    return jax.ShapeDtypeStruct(shape, dtype)


def chunked_call(body, name, row_total, in_specs, out_specs, out_shape, scratch, flops):
    return pl.pallas_call(
        body,
        grid=(row_total // ROW_BLOCK,),
        in_specs=[SMEM] * 3 + in_specs,
        out_specs=out_specs,
        out_shape=out_shape,
        scratch_shapes=scratch,
        compiler_params=pltpu.CompilerParams(vmem_limit_bytes=VMEM_LIMIT),
        cost_estimate=pl.CostEstimate(
            flops=flops, bytes_accessed=1 << 22, transcendentals=0
        ),
        name=name,
    )


def small_call(body, name, out_shape, n_ctx):
    vmem = pl.BlockSpec(memory_space=pltpu.VMEM)
    return pl.pallas_call(
        body,
        in_specs=[SMEM, vmem],
        out_specs=vmem,
        out_shape=out_shape,
        scratch_shapes=[pltpu.SMEM((n_ctx,), jnp.int32)],
        name=name,
    )


def on_device(queries, keys, values, grad_out, lengths, tile_of):
    tile_rows, heads, width = queries.shape
    n_ctx = lax.axis_size("ctx")
    n_head = lax.axis_size("head")
    n_all = n_ctx * n_head
    piece = tile_rows // n_all
    both = ("ctx", "head")
    most_doc = n_ctx * tile_rows // 8
    window = -(-(most_doc - 1) // tile_rows)
    past_rows = window * tile_rows
    row_total = tile_rows * heads
    place = lax.axis_index("ctx").astype(jnp.int32).reshape(1)
    y = lax.axis_index("head")
    scalars = (place, lengths, tile_of)
    q_rows = queries.reshape(row_total, width)
    g_rows = grad_out.reshape(row_total, width)
    work = 2 * row_total * tile_rows * width
    fine = piece % 16 == 0

    def spread(tile):
        pieces = tile.reshape(n_ctx, n_head, piece, width)
        mine = lax.dynamic_index_in_dim(pieces, y, 1, keepdims=False)
        return lax.all_to_all(mine, "ctx", 0, 0, tiled=True)

    def fetch(held):
        packed = small_call(
            functools.partial(route_kernel, window),
            "route",
            shape_of((n_ctx, n_head, window, piece, width), BF16),
            n_ctx,
        )(tile_of, held)
        past = lax.all_to_all(
            packed.reshape(n_all, window, piece, width), both, 0, 0, tiled=True
        )
        if not fine:
            past = past.transpose(1, 0, 2, 3).reshape(1, window, tile_rows, width)
        return past

    pieces_shape = (n_all, window, piece, width) if fine else (1, window, tile_rows, width)

    def send_back(terms):
        if not fine:
            terms = terms.reshape(window, n_all, piece, width).transpose(1, 0, 2, 3)
        terms = lax.all_to_all(terms, both, 0, 0, tiled=True)
        summed = small_call(
            functools.partial(sum_kernel, window),
            "sum_terms",
            shape_of((n_ctx, n_head, piece, width), BF16),
            n_ctx,
        )(tile_of, terms.reshape(n_ctx, n_head, window, piece, width))
        result = lax.all_to_all(
            summed.reshape(n_all, piece, width), both, 0, 0, tiled=True
        )
        return result.reshape(tile_rows, width)

    held_keys = spread(keys)
    held_values = spread(values)
    past_keys = fetch(held_keys)
    past_values = fetch(held_values)

    q_turned, g_turned, own_weight, own_out, own_stats = chunked_call(
        functools.partial(own_forward_kernel, heads),
        "own_forward",
        row_total,
        [rows_of(width), rows_of(width), whole((tile_rows, width)), whole((tile_rows, width))],
        (
            columns_of(width),
            columns_of(width),
            columns_of(tile_rows),
            columns_of(width),
            columns_of(8),
        ),
        (
            shape_of((width, row_total), BF16),
            shape_of((width, row_total), BF16),
            shape_of((tile_rows, row_total), BF16),
            shape_of((width, row_total), F32),
            shape_of((8, row_total), F32),
        ),
        [pltpu.VMEM((width, tile_rows), BF16), pltpu.VMEM((tile_rows, ROW_BLOCK), F32)],
        2 * work,
    )(*scalars, q_rows, g_rows, keys, values)

    prob, stats, dv_terms = chunked_call(
        functools.partial(past_weights_kernel, window, heads, tile_rows),
        "past_weights",
        row_total,
        [columns_of(width), rows_of(width), columns_of(8), whole(pieces_shape)],
        (columns_of(past_rows), columns_of(8), whole(pieces_shape)),
        (
            shape_of((past_rows, row_total), BF16),
            shape_of((8, row_total), F32),
            shape_of(pieces_shape, BF16),
        ),
        [
            pltpu.VMEM((past_rows, width), BF16),
            pltpu.VMEM((past_rows, ROW_BLOCK), F32),
            pltpu.VMEM((past_rows, width), F32),
        ],
        2 * window * work,
    )(*scalars, q_turned, g_rows, own_stats, past_keys)

    attended, delta, past_dq, dk_terms = chunked_call(
        functools.partial(past_grads_kernel, window, heads, tile_rows),
        "past_grads",
        row_total,
        [
            rows_of(width),
            columns_of(width),
            columns_of(past_rows),
            columns_of(8),
            columns_of(width),
            whole(pieces_shape),
            whole(pieces_shape),
        ],
        (rows_of(width), columns_of(8), columns_of(width), whole(pieces_shape)),
        (
            shape_of((row_total, width), BF16),
            shape_of((8, row_total), F32),
            shape_of((width, row_total), F32),
            shape_of(pieces_shape, BF16),
        ),
        [
            pltpu.VMEM((past_rows, width), BF16),
            pltpu.VMEM((past_rows, width), BF16),
            pltpu.VMEM((width, past_rows), BF16),
            pltpu.VMEM((width, past_rows), BF16),
            pltpu.VMEM((past_rows, width), F32),
        ],
        4 * window * work,
    )(*scalars, q_rows, g_turned, prob, stats, own_out, past_keys, past_values)

    query_grad, own_grads = chunked_call(
        functools.partial(own_grads_kernel, heads),
        "own_grads",
        row_total,
        [
            rows_of(width),
            rows_of(width),
            columns_of(width),
            columns_of(tile_rows),
            columns_of(8),
            columns_of(8),
            columns_of(width),
            whole((tile_rows, width)),
            whole((tile_rows, width)),
        ],
        (rows_of(width), whole((2, tile_rows, width))),
        (
            shape_of((row_total, width), BF16),
            shape_of((2, tile_rows, width), BF16),
        ),
        [
            pltpu.VMEM((width, tile_rows), BF16),
            pltpu.VMEM((tile_rows, width), F32),
            pltpu.VMEM((tile_rows, width), F32),
        ],
        4 * work,
    )(*scalars, q_rows, g_rows, g_turned, own_weight, stats, delta, past_dq, keys, values)

    far_values = send_back(dv_terms)
    far_keys = send_back(dk_terms)
    if n_head == 2:
        peer = lax.ppermute(own_grads, "head", [(0, 1), (1, 0)])
        near = own_grads.astype(F32) + peer.astype(F32)
    else:
        near = lax.psum(own_grads.astype(F32), "head")
    return (
        attended.reshape(tile_rows, heads, width),
        query_grad.reshape(tile_rows, heads, width),
        near[0] + far_keys.astype(F32),
        near[1] + far_values.astype(F32),
    )


def solution(mesh):
    return jax.shard_map(
        on_device,
        mesh=mesh,
        in_specs=(
            P("ctx", "head", None),
            P("ctx", None),
            P("ctx", None),
            P("ctx", "head", None),
            P(),
            P(),
        ),
        out_specs=(P("ctx", "head", None), P("ctx", "head", None), P("ctx", None), P("ctx", None)),
        check_vma=False,
    )
```

```python
import functools

import jax
import jax.numpy as jnp
from jax import lax
from jax.experimental import pallas as pl
from jax.experimental.pallas import tpu as pltpu
from jax.sharding import PartitionSpec as P

LOG2E = 1.4426950408889634
NEG_FILL = -1e30
KEY_BLOCK = 128
ROW_BLOCK = 512
VMEM_LIMIT = 60 * 1024 * 1024
SMEM = pl.BlockSpec(memory_space=pltpu.SMEM)
F32 = jnp.float32
BF16 = jnp.bfloat16


def matmul(left, right):
    return lax.dot_general(left, right, (((1,), (0,)), ((), ())), preferred_element_type=F32)


def fold_rows(block, combine):
    folded = block[0:8]
    for begin in range(8, block.shape[0], 8):
        folded = combine(folded, block[begin : begin + 8])
    return folded


def document_starts(ends, positions):
    start = jnp.zeros_like(positions)
    for end in ends:
        start = jnp.where(end <= positions, end, start)
    return start


def document_ends(lengths_ref):
    ends = []
    total = jnp.int32(0)
    for doc in range(lengths_ref.shape[0]):
        total = total + lengths_ref[doc]
        ends.append(total)
    return ends


def lane_positions(heads, first_pos):
    lane = lax.broadcasted_iota(jnp.int32, (1, ROW_BLOCK), 1)
    return first_pos + lax.div(lane, heads)


def key_positions(begin):
    return begin + lax.broadcasted_iota(jnp.int32, (KEY_BLOCK, ROW_BLOCK), 0)


def fold_all(blocks, combine):
    folded = fold_rows(blocks[0], combine)
    for block in blocks[1:]:
        folded = combine(folded, fold_rows(block, combine))
    return folded


def own_extents(heads, tile_rows):
    chunk_pos = ROW_BLOCK // heads
    ends = [-(-(begin + chunk_pos) // KEY_BLOCK) for begin in range(0, tile_rows, chunk_pos)]
    return sorted(set(ends))


def by_extent(heads, tile_rows, branch):
    chunk_pos = ROW_BLOCK // heads
    extents = own_extents(heads, tile_rows)
    end = lax.div((pl.program_id(0) + 1) * chunk_pos - 1, KEY_BLOCK) + 1
    for extent in extents:
        pl.when(end == extent)(functools.partial(branch, extent))


def own_forward_kernel(
    heads,
    place_ref,
    lengths_ref,
    tile_of_ref,
    q_ref,
    g_ref,
    k_ref,
    v_ref,
    q_turned_ref,
    g_turned_ref,
    weight_ref,
    out_ref,
    stats_ref,
    v_turned,
):
    tile_rows, width = k_ref.shape
    exponent_scale = float(width) ** (-0.5) * LOG2E

    @pl.when(pl.program_id(0) == 0)
    def turn_values():
        v_turned[...] = v_ref[...].T

    tile_begin = tile_of_ref[place_ref[0]] * tile_rows
    first_pos = tile_begin + pl.program_id(0) * (ROW_BLOCK // heads)
    q_turned = q_ref[...].T
    q_turned_ref[...] = q_turned
    g_turned_ref[...] = g_ref[...].T
    q_pos = lane_positions(heads, first_pos)
    low = document_starts(document_ends(lengths_ref), q_pos) - tile_begin
    high = q_pos - tile_begin

    def branch(extent):
        scores = []
        for block in range(extent):
            begin = block * KEY_BLOCK
            score = matmul(k_ref[begin : begin + KEY_BLOCK, :], q_turned)
            key_pos = key_positions(begin)
            live = key_pos >= low
            if block == extent - 1:
                live = live & (key_pos <= high)
            scores.append(jnp.where(live, score, NEG_FILL))
        top = jnp.max(fold_all(scores, jnp.maximum), axis=0, keepdims=True) * exponent_scale
        weights = [jnp.exp2(score * exponent_scale - top) for score in scores]
        out_turned = jnp.zeros((width, ROW_BLOCK), F32)
        for block in range(extent):
            begin = block * KEY_BLOCK
            weight_low = weights[block].astype(BF16)
            weight_ref[begin : begin + KEY_BLOCK, :] = weight_low
            out_turned += matmul(v_turned[:, begin : begin + KEY_BLOCK], weight_low)
        out_ref[...] = out_turned
        stats_ref[0:1, :] = top
        stats_ref[1:2, :] = jnp.sum(fold_all(weights, jnp.add), axis=0, keepdims=True)

    by_extent(heads, tile_rows, branch)


def past_kernel(
    window,
    heads,
    tile_rows,
    place_ref,
    lengths_ref,
    tile_of_ref,
    q_ref,
    g_ref,
    q_turned_ref,
    g_turned_ref,
    own_stats_ref,
    own_out_ref,
    past_ref,
    att_ref,
    dq_ref,
    grads_ref,
    stats_ref,
    k_win,
    v_win,
    k_turned,
    v_turned,
    dk_acc,
    dv_acc,
):
    past_rows, width = k_win.shape
    n_all, _, _, piece, _ = past_ref.shape
    scale = float(width) ** (-0.5)
    exponent_scale = scale * LOG2E
    step = pl.program_id(0)

    @pl.when(step == 0)
    def begin():
        for slot in range(window):
            for owner in range(n_all):
                row = slot * tile_rows + owner * piece
                k_win[row : row + piece, :] = past_ref[owner, slot, 0]
                v_win[row : row + piece, :] = past_ref[owner, slot, 1]
        k_turned[...] = k_win[...].T
        v_turned[...] = v_win[...].T
        dk_acc[...] = jnp.zeros_like(dk_acc)
        dv_acc[...] = jnp.zeros_like(dv_acc)

    base = (tile_of_ref[place_ref[0]] - window) * tile_rows
    first_pos = base + past_rows + step * (ROW_BLOCK // heads)
    ends = document_ends(lengths_ref)
    first_start = jnp.maximum(document_starts(ends, first_pos) - base, 0)
    unit = window * KEY_BLOCK
    branches = past_rows // unit
    live_units = branches - lax.div(jnp.minimum(first_start, past_rows), unit)
    low = document_starts(ends, lane_positions(heads, first_pos)) - base
    own_top = own_stats_ref[0:1, :]
    own_sum = own_stats_ref[1:2, :]

    def finish_chunk(out_turned, dq_turned, rescale, delta):
        att_ref[...] = out_turned.T.astype(BF16)
        dq_ref[...] = dq_turned
        stats_ref[0:1, :] = rescale
        stats_ref[1:2, :] = delta

    def branch(units):
        q_turned = q_turned_ref[...]
        g_turned = g_turned_ref[...]
        begins = range(past_rows - units * unit, past_rows, KEY_BLOCK)
        scores = []
        for begin in begins:
            score = matmul(k_win[begin : begin + KEY_BLOCK, :], q_turned)
            scores.append(jnp.where(key_positions(begin) >= low, score, NEG_FILL))
        top = jnp.max(fold_all(scores, jnp.maximum), axis=0, keepdims=True) * exponent_scale
        top = jnp.maximum(top, own_top)
        weights = [jnp.exp2(score * exponent_scale - top) for score in scores]
        dprobs = [matmul(v_win[begin : begin + KEY_BLOCK, :], g_turned) for begin in begins]
        rescale = jnp.exp2(own_top - top)
        total = own_sum * rescale + jnp.sum(
            fold_all(weights, jnp.add), axis=0, keepdims=True
        )
        inverse = 1.0 / total
        rescale = rescale * inverse
        out_turned = own_out_ref[...] * rescale
        probs = [weight * inverse for weight in weights]
        for begin, prob in zip(begins, probs):
            prob_low = prob.astype(BF16)
            out_turned += matmul(v_turned[:, begin : begin + KEY_BLOCK], prob_low)
            dv_acc[begin : begin + KEY_BLOCK, :] += matmul(prob_low, g_ref[...])
        delta = jnp.sum(out_turned * g_turned.astype(F32), axis=0, keepdims=True)
        dq_turned = jnp.zeros((width, ROW_BLOCK), F32)
        for begin, prob, dprob in zip(begins, probs, dprobs):
            dscore = (prob * (dprob - delta)).astype(BF16)
            dk_acc[begin : begin + KEY_BLOCK, :] += matmul(dscore, q_ref[...])
            dq_turned += matmul(k_turned[:, begin : begin + KEY_BLOCK], dscore)
        finish_chunk(out_turned, dq_turned, rescale, delta)

    @pl.when(live_units == 0)
    def nothing_past():
        rescale = 1.0 / own_sum
        out_turned = own_out_ref[...] * rescale
        delta = jnp.sum(out_turned * g_turned_ref[...].astype(F32), axis=0, keepdims=True)
        finish_chunk(out_turned, jnp.zeros((width, ROW_BLOCK), F32), rescale, delta)

    for units in range(1, branches + 1):
        pl.when(live_units == units)(functools.partial(branch, units))

    @pl.when(step == pl.num_programs(0) - 1)
    def finish():
        for slot in range(window):
            for owner in range(n_all):
                row = slot * tile_rows + owner * piece
                grads_ref[owner, slot, 0] = (dk_acc[row : row + piece, :] * scale).astype(BF16)
                grads_ref[owner, slot, 1] = dv_acc[row : row + piece, :].astype(BF16)


def own_grads_kernel(
    heads,
    q_ref,
    g_ref,
    g_turned_ref,
    weight_ref,
    stats_ref,
    past_dq_ref,
    k_ref,
    v_ref,
    dq_ref,
    dkv_ref,
    k_turned,
    dk_acc,
    dv_acc,
):
    tile_rows, width = k_ref.shape
    scale = float(width) ** (-0.5)

    @pl.when(pl.program_id(0) == 0)
    def begin():
        k_turned[...] = k_ref[...].T
        dk_acc[...] = jnp.zeros_like(dk_acc)
        dv_acc[...] = jnp.zeros_like(dv_acc)

    rescale = stats_ref[0:1, :]
    delta = stats_ref[1:2, :]

    def branch(extent):
        q_rows = q_ref[...]
        g_rows = g_ref[...]
        g_turned = g_turned_ref[...]
        dq_turned = past_dq_ref[...]
        for block in range(extent):
            begin = block * KEY_BLOCK
            keys = slice(begin, begin + KEY_BLOCK)
            prob = weight_ref[keys, :].astype(F32) * rescale
            dprob = matmul(v_ref[keys, :], g_turned)
            dscore = (prob * (dprob - delta)).astype(BF16)
            dv_acc[keys, :] += matmul(prob.astype(BF16), g_rows)
            dk_acc[keys, :] += matmul(dscore, q_rows)
            dq_turned += matmul(k_turned[:, keys], dscore)
        dq_ref[...] = (dq_turned * scale).T.astype(BF16)

    by_extent(heads, tile_rows, branch)

    @pl.when(pl.program_id(0) == pl.num_programs(0) - 1)
    def finish():
        dkv_ref[0] = (dk_acc[...] * scale).astype(BF16)
        dkv_ref[1] = dv_acc[...].astype(BF16)


def route_kernel(window, tile_of_ref, held_ref, out_ref, holder):
    n_ctx, n_head = out_ref.shape[:2]
    for ctx in range(n_ctx):
        holder[tile_of_ref[ctx]] = ctx

    def one(ctx, carry):
        for slot in range(window):
            tile = tile_of_ref[ctx] - (window - slot)
            source = holder[jnp.maximum(tile, 0)]
            rows = held_ref[source]
            for head in range(n_head):
                out_ref[ctx, head, slot] = rows
        return carry

    lax.fori_loop(0, n_ctx, one, 0)


def sum_kernel(window, tile_of_ref, terms_ref, out_ref, holder):
    n_ctx, n_head = out_ref.shape[:2]
    for ctx in range(n_ctx):
        holder[tile_of_ref[ctx]] = ctx

    def one(ctx, carry):
        total = jnp.zeros(out_ref.shape[2:], F32)
        for slot in range(window):
            tile = tile_of_ref[ctx] + (window - slot)
            source = holder[jnp.minimum(tile, n_ctx - 1)]
            part = terms_ref[source, 0, slot].astype(F32)
            for head in range(1, n_head):
                part = part + terms_ref[source, head, slot].astype(F32)
            total = total + jnp.where(tile < n_ctx, part, 0.0)
        for head in range(n_head):
            out_ref[ctx, head] = total.astype(BF16)
        return carry

    lax.fori_loop(0, n_ctx, one, 0)


def whole(shape):
    return pl.BlockSpec(shape, lambda chunk: (0,) * len(shape))


def rows_of(width):
    return pl.BlockSpec((ROW_BLOCK, width), lambda chunk: (chunk, 0))


def columns_of(height):
    return pl.BlockSpec((height, ROW_BLOCK), lambda chunk: (0, chunk))


def shape_of(shape, dtype):
    return jax.ShapeDtypeStruct(shape, dtype)


def chunked_call(body, name, scalars, row_total, in_specs, out_specs, out_shape, scratch, flops):
    return pl.pallas_call(
        body,
        grid=(row_total // ROW_BLOCK,),
        in_specs=[SMEM] * scalars + in_specs,
        out_specs=out_specs,
        out_shape=out_shape,
        scratch_shapes=scratch,
        compiler_params=pltpu.CompilerParams(vmem_limit_bytes=VMEM_LIMIT),
        cost_estimate=pl.CostEstimate(
            flops=flops, bytes_accessed=1 << 22, transcendentals=0
        ),
        name=name,
    )


def small_call(body, name, out_shape, n_ctx):
    vmem = pl.BlockSpec(memory_space=pltpu.VMEM)
    return pl.pallas_call(
        body,
        in_specs=[SMEM, vmem],
        out_specs=vmem,
        out_shape=out_shape,
        scratch_shapes=[pltpu.SMEM((n_ctx,), jnp.int32)],
        compiler_params=pltpu.CompilerParams(vmem_limit_bytes=VMEM_LIMIT),
        name=name,
    )


def on_device(queries, keys, values, grad_out, lengths, tile_of):
    tile_rows, heads, width = queries.shape
    n_ctx = lax.axis_size("ctx")
    n_head = lax.axis_size("head")
    n_all = n_ctx * n_head
    piece = tile_rows // n_all
    both = ("ctx", "head")
    most_doc = n_ctx * tile_rows // 8
    window = -(-(most_doc - 1) // tile_rows)
    past_rows = window * tile_rows
    row_total = tile_rows * heads
    place = lax.axis_index("ctx").astype(jnp.int32).reshape(1)
    y = lax.axis_index("head")
    scalars = (place, lengths, tile_of)
    q_rows = queries.reshape(row_total, width)
    g_rows = grad_out.reshape(row_total, width)
    work = 2 * row_total * tile_rows * width
    fine = piece % 16 == 0

    pieces = jnp.stack(
        [tile.reshape(n_ctx, n_head, piece, width) for tile in (keys, values)], axis=2
    )
    mine = lax.dynamic_index_in_dim(pieces, y, 1, keepdims=False)
    held = lax.all_to_all(mine, "ctx", 0, 0, tiled=True)
    packed = small_call(
        functools.partial(route_kernel, window),
        "route",
        shape_of((n_ctx, n_head, window, 2, piece, width), BF16),
        n_ctx,
    )(tile_of, held)
    past = lax.all_to_all(
        packed.reshape(n_all, window, 2, piece, width), both, 0, 0, tiled=True
    )
    pieces_shape = (n_all, window, 2, piece, width)
    if not fine:
        pieces_shape = (1, window, 2, tile_rows, width)
        past = past.transpose(1, 2, 0, 3, 4).reshape(pieces_shape)

    q_turned, g_turned, own_weight, own_out, own_stats = chunked_call(
        functools.partial(own_forward_kernel, heads),
        "own_forward",
        3,
        row_total,
        [rows_of(width), rows_of(width), whole((tile_rows, width)), whole((tile_rows, width))],
        (
            columns_of(width),
            columns_of(width),
            columns_of(tile_rows),
            columns_of(width),
            columns_of(8),
        ),
        (
            shape_of((width, row_total), BF16),
            shape_of((width, row_total), BF16),
            shape_of((tile_rows, row_total), BF16),
            shape_of((width, row_total), F32),
            shape_of((8, row_total), F32),
        ),
        [pltpu.VMEM((width, tile_rows), BF16)],
        2 * work,
    )(*scalars, q_rows, g_rows, keys, values)

    attended, past_dq, terms, stats = chunked_call(
        functools.partial(past_kernel, window, heads, tile_rows),
        "past",
        3,
        row_total,
        [
            rows_of(width),
            rows_of(width),
            columns_of(width),
            columns_of(width),
            columns_of(8),
            columns_of(width),
            whole(pieces_shape),
        ],
        (rows_of(width), columns_of(width), whole(pieces_shape), columns_of(8)),
        (
            shape_of((row_total, width), BF16),
            shape_of((width, row_total), F32),
            shape_of(pieces_shape, BF16),
            shape_of((8, row_total), F32),
        ),
        [
            pltpu.VMEM((past_rows, width), BF16),
            pltpu.VMEM((past_rows, width), BF16),
            pltpu.VMEM((width, past_rows), BF16),
            pltpu.VMEM((width, past_rows), BF16),
            pltpu.VMEM((past_rows, width), F32),
            pltpu.VMEM((past_rows, width), F32),
        ],
        6 * window * work,
    )(*scalars, q_rows, g_rows, q_turned, g_turned, own_stats, own_out, past)

    query_grad, own_grads = chunked_call(
        functools.partial(own_grads_kernel, heads),
        "own_grads",
        0,
        row_total,
        [
            rows_of(width),
            rows_of(width),
            columns_of(width),
            columns_of(tile_rows),
            columns_of(8),
            columns_of(width),
            whole((tile_rows, width)),
            whole((tile_rows, width)),
        ],
        (rows_of(width), whole((2, tile_rows, width))),
        (
            shape_of((row_total, width), BF16),
            shape_of((2, tile_rows, width), BF16),
        ),
        [
            pltpu.VMEM((width, tile_rows), BF16),
            pltpu.VMEM((tile_rows, width), F32),
            pltpu.VMEM((tile_rows, width), F32),
        ],
        4 * work,
    )(q_rows, g_rows, g_turned, own_weight, stats, past_dq, keys, values)

    if not fine:
        terms = terms.reshape(window, 2, n_all, piece, width).transpose(2, 0, 1, 3, 4)
    terms = lax.all_to_all(terms, both, 0, 0, tiled=True)
    summed = small_call(
        functools.partial(sum_kernel, window),
        "sum_terms",
        shape_of((n_ctx, n_head, 2, piece, width), BF16),
        n_ctx,
    )(tile_of, terms.reshape(n_ctx, n_head, window, 2, piece, width))
    far = lax.all_to_all(summed.reshape(n_all, 2, piece, width), both, 0, 0, tiled=True)
    if n_head == 2:
        peer = lax.ppermute(own_grads, "head", [(0, 1), (1, 0)])
        near = own_grads.astype(F32) + peer.astype(F32)
    else:
        near = lax.psum(own_grads.astype(F32), "head")
    far_keys, far_values = (
        far[:, part].reshape(tile_rows, width).astype(F32) for part in range(2)
    )
    return (
        attended.reshape(tile_rows, heads, width),
        query_grad.reshape(tile_rows, heads, width),
        near[0] + far_keys,
        near[1] + far_values,
    )


def solution(mesh):
    return jax.shard_map(
        on_device,
        mesh=mesh,
        in_specs=(
            P("ctx", "head", None),
            P("ctx", None),
            P("ctx", None),
            P("ctx", "head", None),
            P(),
            P(),
        ),
        out_specs=(P("ctx", "head", None), P("ctx", "head", None), P("ctx", None), P("ctx", None)),
        check_vma=False,
    )
```

```python
import functools

import jax
import jax.numpy as jnp
from jax import lax
from jax.experimental import pallas as pl
from jax.experimental.pallas import tpu as pltpu
from jax.sharding import PartitionSpec as P

LOG2E = 1.4426950408889634
NEG_FILL = -1e30
KEY_BLOCK = 256
ROW_BLOCK = 1024
VMEM_LIMIT = 60 * 1024 * 1024
SMALL_LIMIT = 16 * 1024 * 1024
SMEM = pl.BlockSpec(memory_space=pltpu.SMEM)
VMEM = pl.BlockSpec(memory_space=pltpu.VMEM)
HBM = pl.BlockSpec(memory_space=pl.ANY)
F32 = jnp.float32
BF16 = jnp.bfloat16


def matmul(left, right):
    return lax.dot_general(left, right, (((1,), (0,)), ((), ())), preferred_element_type=F32)


def matmul_first(left, right):
    return lax.dot_general(left, right, (((0,), (0,)), ((), ())), preferred_element_type=F32)


def matmul_last(left, right):
    return lax.dot_general(left, right, (((1,), (1,)), ((), ())), preferred_element_type=F32)


def fold_rows(block, combine):
    folded = block[0:8]
    for begin in range(8, block.shape[0], 8):
        folded = combine(folded, block[begin : begin + 8])
    return folded


def document_starts(ends, positions):
    start = jnp.zeros_like(positions)
    for end in ends:
        start = jnp.where(end <= positions, end, start)
    return start


def document_ends(lengths_ref):
    ends = []
    total = jnp.int32(0)
    for doc in range(lengths_ref.shape[0]):
        total = total + lengths_ref[doc]
        ends.append(total)
    return ends


def lane_positions(heads, first_pos):
    lane = lax.broadcasted_iota(jnp.int32, (1, ROW_BLOCK), 1)
    return first_pos + lax.div(lane, heads)


def key_positions(keys):
    shape = (keys.stop - keys.start, ROW_BLOCK)
    return keys.start + lax.broadcasted_iota(jnp.int32, shape, 0)


def fold_all(blocks, combine):
    folded = fold_rows(blocks[0], combine)
    for block in blocks[1:]:
        folded = combine(folded, fold_rows(block, combine))
    return folded


def row_blocks(total):
    return [slice(begin, begin + ROW_BLOCK) for begin in range(0, total, ROW_BLOCK)]


def key_blocks(begin, end):
    starts = list(range(end - KEY_BLOCK, begin, -KEY_BLOCK))[::-1]
    starts = [begin] + [start for start in starts if start > begin]
    return [slice(start, stop) for start, stop in zip(starts, starts[1:] + [end])]


def own_forward_kernel(
    heads, place_ref, lengths_ref, tile_of_ref, q_ref, g_ref, k_ref, v_ref, stats_ref, *weight_refs
):
    tile_rows, width = k_ref.shape
    exponent_scale = float(width) ** (-0.5) * LOG2E
    chunk_pos = ROW_BLOCK // heads
    tile_begin = tile_of_ref[place_ref[0]] * tile_rows
    ends = document_ends(lengths_ref)

    for chunk, rows in enumerate(row_blocks(q_ref.shape[0])):
        first_pos = tile_begin + chunk * chunk_pos
        q_pos = lane_positions(heads, first_pos)
        low = document_starts(ends, q_pos) - tile_begin
        high = q_pos - tile_begin
        blocks = key_blocks(0, (chunk + 1) * chunk_pos)
        scores = []
        for keys in blocks:
            score = matmul_last(k_ref[keys, :], q_ref[rows, :])
            key_pos = key_positions(keys)
            live = key_pos >= low
            if keys.stop > chunk * chunk_pos:
                live = live & (key_pos <= high)
            scores.append(jnp.where(live, score, NEG_FILL))
        top = jnp.max(fold_all(scores, jnp.maximum), axis=0, keepdims=True) * exponent_scale
        sums = jnp.zeros((8, ROW_BLOCK), F32)
        products = jnp.zeros((8, ROW_BLOCK), F32)
        for keys, score in zip(blocks, scores):
            weight = jnp.exp2(score * exponent_scale - top)
            weight_refs[chunk][keys, :] = weight.astype(BF16)
            dprob = matmul_last(v_ref[keys, :], g_ref[rows, :])
            sums += fold_rows(weight, jnp.add)
            products += fold_rows(weight * dprob, jnp.add)
        stats_ref[0:1, rows] = top
        stats_ref[1:2, rows] = jnp.sum(sums, axis=0, keepdims=True)
        stats_ref[2:3, rows] = jnp.sum(products, axis=0, keepdims=True)


class Past:
    def __init__(self, window, heads, place_ref, lengths_ref, tile_of_ref, past_hbm, win_ref):
        n_owners, _, _, self.piece, self.width = past_hbm.shape
        self.n_owners = n_owners
        self.tile_rows = n_owners * self.piece
        self.past_rows = window * self.tile_rows
        self.chunk_pos = ROW_BLOCK // heads
        self.heads = heads
        self.window = window
        self.past_hbm = past_hbm
        self.win_ref = win_ref
        self.tile_begin = tile_of_ref[place_ref[0]] * self.tile_rows
        first_start, self.first_end = jnp.int32(0), jnp.int32(0)
        for end in document_ends(lengths_ref):
            crosses = (self.first_end <= self.tile_begin) & (end > self.tile_begin)
            first_start = jnp.where(end <= self.tile_begin, end, first_start)
            self.first_end = jnp.where(crosses, end, self.first_end)
        self.first_key = jnp.maximum(self.past_rows - (self.tile_begin - first_start), 0)
        self.unit = window * KEY_BLOCK // 4
        self.branches = self.past_rows // self.unit
        self.all_units = self.branches - lax.div(self.first_key, self.unit)

    def copies(self, part, sem):
        return [
            pltpu.make_async_copy(
                self.past_hbm.at[:, slot, part],
                self.win_ref.at[part, slot],
                sem.at[part, slot],
            )
            for slot in range(self.window)
        ]

    def rows(self, part, keys):
        slot, begin = divmod(keys.start, self.tile_rows)
        end = begin + keys.stop - keys.start
        if end > self.tile_rows:
            border = (slot + 1) * self.tile_rows
            parts = [
                self.rows(part, slice(keys.start, border)),
                self.rows(part, slice(border, keys.stop)),
            ]
            return jnp.concatenate(parts, axis=0)
        if self.n_owners == 1:
            return self.win_ref[part, slot, 0, begin:end, :]
        rows = self.win_ref[part, slot, begin // self.piece : end // self.piece]
        return rows.reshape(end - begin, self.width)

    def scores(self, units, q_rows):
        blocks = key_blocks(self.past_rows - units * self.unit, self.past_rows)
        scores = [matmul_last(self.rows(0, keys), q_rows) for keys in blocks]
        live = key_positions(blocks[0]) >= self.first_key
        scores[0] = jnp.where(live, scores[0], NEG_FILL)
        return blocks, scores

    def by_units(self, chunk, nothing, branch):
        first_pos = self.tile_begin + chunk * self.chunk_pos
        live_units = jnp.where(first_pos < self.first_end, self.all_units, 0)
        pl.when(live_units == 0)(nothing)
        for units in range(1, self.branches + 1):
            pl.when(live_units == units)(functools.partial(branch, units))

    def has_past(self, chunk):
        first_pos = self.tile_begin + chunk * self.chunk_pos
        return lane_positions(self.heads, first_pos) < self.first_end


def chunk_rows(chunk):
    return pl.ds(pl.multiple_of(chunk * ROW_BLOCK, ROW_BLOCK), ROW_BLOCK)


def chunk_copies(pairs, sem, chunk):
    rows = chunk_rows(chunk)
    copies = []
    for index, (source, target, axis) in enumerate(pairs):
        where = (rows, slice(None)) if axis == 0 else (slice(None), rows)
        copies.append(
            pltpu.make_async_copy(source.at[where], target.at[where], sem.at[chunk, index])
        )
    return copies


def start_all(copies):
    for copy in copies:
        copy.start()


def wait_all(copies):
    for copy in copies:
        copy.wait()


def past_kernel(
    window,
    heads,
    place_ref,
    lengths_ref,
    tile_of_ref,
    q_hbm,
    g_hbm,
    own_stats_hbm,
    past_hbm,
    stats_hbm,
    terms_hbm,
    q_ref,
    g_ref,
    own_stats_ref,
    stats_ref,
    win_ref,
    terms_ref,
    dk_acc,
    dv_acc,
    in_sem,
    past_sem,
    stats_sem,
    terms_sem,
):
    past = Past(window, heads, place_ref, lengths_ref, tile_of_ref, past_hbm, win_ref)
    past_rows, width = dk_acc.shape
    scale = float(width) ** (-0.5)
    exponent_scale = scale * LOG2E
    chunks = q_ref.shape[0] // ROW_BLOCK
    pairs = ((q_hbm, q_ref, 0), (g_hbm, g_ref, 0))
    stats_in = pltpu.make_async_copy(own_stats_hbm, own_stats_ref, stats_sem.at[0])
    stats_out = pltpu.make_async_copy(stats_ref, stats_hbm, stats_sem.at[1])

    start_all(past.copies(0, past_sem))
    start_all(chunk_copies(pairs, in_sem, 0))
    stats_in.start()
    start_all(past.copies(1, past_sem))
    for chunk in range(1, chunks):
        start_all(chunk_copies(pairs, in_sem, chunk))
    dk_acc[...] = jnp.zeros_like(dk_acc)
    dv_acc[...] = jnp.zeros_like(dv_acc)
    wait_all(past.copies(0, past_sem) + past.copies(1, past_sem) + [stats_in])

    def chunk_step(chunk, carry):
        rows = chunk_rows(chunk)
        wait_all(chunk_copies(pairs, in_sem, chunk))
        own_top = own_stats_ref[0:1, rows]
        own_sum = own_stats_ref[1:2, rows]
        own_product = own_stats_ref[2:3, rows]

        def branch(units):
            has_past = past.has_past(chunk)
            q_rows = q_ref[rows, :]
            g_rows = g_ref[rows, :]
            blocks, scores = past.scores(units, q_rows)
            dprobs = [matmul_last(past.rows(1, keys), g_rows) for keys in blocks]
            top = jnp.max(fold_all(scores, jnp.maximum), axis=0, keepdims=True)
            top = jnp.where(has_past, jnp.maximum(top * exponent_scale, own_top), own_top)
            shift = jnp.where(has_past, top, -NEG_FILL)
            sums = jnp.zeros((8, ROW_BLOCK), F32)
            products = jnp.zeros((8, ROW_BLOCK), F32)
            weights = []
            for score, dprob in zip(scores, dprobs):
                weight = jnp.exp2(score * exponent_scale - shift)
                sums += fold_rows(weight, jnp.add)
                products += fold_rows(weight * dprob, jnp.add)
                weights.append(weight.astype(BF16))
            rescale = jnp.exp2(own_top - top)
            total = own_sum * rescale + jnp.sum(sums, axis=0, keepdims=True)
            product = own_product * rescale + jnp.sum(products, axis=0, keepdims=True)
            inverse = 1.0 / total
            delta = product * inverse
            stats_ref[0:1, rows] = rescale * inverse
            stats_ref[1:2, rows] = delta
            stats_ref[2:3, rows] = jnp.where(has_past, top + jnp.log2(total), -NEG_FILL)
            inverse_low = inverse.astype(BF16)
            probs = [weight * inverse_low for weight in weights]
            for keys, prob in zip(blocks, probs):
                dv_acc[keys, :] += matmul(prob, g_rows)
            for keys, prob, dprob in zip(blocks, probs, dprobs):
                dscore = prob * (dprob - delta).astype(BF16)
                dk_acc[keys, :] += matmul(dscore, q_rows)

        def nothing():
            inverse = 1.0 / own_sum
            stats_ref[0:1, rows] = inverse
            stats_ref[1:2, rows] = own_product * inverse
            stats_ref[2:3, rows] = jnp.full((1, ROW_BLOCK), -NEG_FILL, F32)

        past.by_units(chunk, nothing, branch)
        return carry

    lax.fori_loop(0, chunks, chunk_step, 0)
    stats_out.start()
    copies = [stats_out]
    for slot in range(window):
        rows = slice(slot * past.tile_rows, (slot + 1) * past.tile_rows)
        shape = (past.n_owners, past.piece, width)
        terms_ref[0, slot] = (dk_acc[rows, :] * scale).astype(BF16).reshape(shape)
        terms_ref[1, slot] = dv_acc[rows, :].astype(BF16).reshape(shape)
        for part in range(2):
            copy = pltpu.make_async_copy(
                terms_ref.at[part, slot], terms_hbm.at[:, slot, part], terms_sem.at[part, slot]
            )
            copy.start()
            copies.append(copy)
    wait_all(copies)


def late_kernel(
    window,
    heads,
    place_ref,
    lengths_ref,
    tile_of_ref,
    q_hbm,
    g_hbm,
    stats_hbm,
    past_hbm,
    own_out_hbm,
    own_dq_hbm,
    summed_hbm,
    att_hbm,
    dq_hbm,
    q_ref,
    g_ref,
    stats_ref,
    win_ref,
    own_out_ref,
    own_dq_ref,
    att_ref,
    dq_ref,
    in_sem,
    past_sem,
    stats_sem,
    out_sem,
):
    past = Past(window, heads, place_ref, lengths_ref, tile_of_ref, past_hbm, win_ref)
    width = past.width
    scale = float(width) ** (-0.5)
    exponent_scale = scale * LOG2E
    chunks = q_ref.shape[0] // ROW_BLOCK
    pairs = (
        (q_hbm, q_ref, 0),
        (g_hbm, g_ref, 0),
        (own_out_hbm, own_out_ref, 1),
        (own_dq_hbm, own_dq_ref, 1),
    )
    out_pairs = ((att_ref, att_hbm, 0), (dq_ref, dq_hbm, 0))
    stats_in = pltpu.make_async_copy(stats_hbm, stats_ref, stats_sem.at[0])
    start_all(past.copies(0, past_sem) + past.copies(1, past_sem) + [stats_in])
    for chunk in range(chunks):
        start_all(chunk_copies(pairs, in_sem, chunk))
    wait_all(past.copies(0, past_sem) + past.copies(1, past_sem) + [stats_in])

    def chunk_step(chunk, carry):
        rows = chunk_rows(chunk)
        wait_all(chunk_copies(pairs, in_sem, chunk))

        def branch(units):
            q_rows = q_ref[rows, :]
            g_rows = g_ref[rows, :]
            delta = stats_ref[1:2, rows]
            shift = stats_ref[2:3, rows]
            blocks, scores = past.scores(units, q_rows)
            out_turned = own_out_ref[:, rows].astype(F32)
            dq_turned = own_dq_ref[:, rows].astype(F32)
            for keys, score in zip(blocks, scores):
                prob = jnp.exp2(score * exponent_scale - shift).astype(BF16)
                out_turned += matmul_first(past.rows(1, keys), prob)
                dprob = matmul_last(past.rows(1, keys), g_rows)
                dscore = prob * (dprob - delta).astype(BF16)
                dq_turned += matmul_first(past.rows(0, keys), dscore)
            att_ref[rows, :] = out_turned.astype(BF16).T
            dq_ref[rows, :] = (dq_turned * scale).astype(BF16).T

        def nothing():
            att_ref[rows, :] = own_out_ref[:, rows].T
            dq_ref[rows, :] = (own_dq_ref[:, rows].astype(F32) * scale).astype(BF16).T

        past.by_units(chunk, nothing, branch)
        start_all(chunk_copies(out_pairs, out_sem, chunk))
        return carry

    lax.fori_loop(0, chunks, chunk_step, 0)
    for chunk in range(chunks):
        wait_all(chunk_copies(out_pairs, out_sem, chunk))


def own_grads_kernel(
    heads, q_ref, g_ref, stats_ref, k_ref, v_ref, *refs
):
    tile_rows, width = k_ref.shape
    chunk_pos = ROW_BLOCK // heads
    chunks = q_ref.shape[0] // ROW_BLOCK
    weight_refs = refs[:chunks]
    out_ref, dq_ref, dkv_ref, dk_acc, dv_acc = refs[chunks:]
    scale = float(width) ** (-0.5)
    dk_acc[...] = jnp.zeros_like(dk_acc)
    dv_acc[...] = jnp.zeros_like(dv_acc)

    for chunk, rows in enumerate(row_blocks(q_ref.shape[0])):
        rescale = stats_ref[0:1, rows]
        delta = stats_ref[1:2, rows]
        q_rows = q_ref[rows, :]
        g_rows = g_ref[rows, :]
        out_turned = jnp.zeros((width, ROW_BLOCK), F32)
        dq_turned = jnp.zeros((width, ROW_BLOCK), F32)
        for keys in key_blocks(0, (chunk + 1) * chunk_pos):
            prob = (weight_refs[chunk][keys, :].astype(F32) * rescale).astype(BF16)
            dprob = matmul_last(v_ref[keys, :], g_rows)
            dscore = prob * (dprob - delta).astype(BF16)
            dv_acc[keys, :] += matmul(prob, g_rows)
            dk_acc[keys, :] += matmul(dscore, q_rows)
            out_turned += matmul_first(v_ref[keys, :], prob)
            dq_turned += matmul_first(k_ref[keys, :], dscore)
        out_ref[:, rows] = out_turned.astype(BF16)
        dq_ref[:, rows] = dq_turned.astype(BF16)

    dkv_ref[0] = (dk_acc[...] * scale).astype(BF16)
    dkv_ref[1] = dv_acc[...].astype(BF16)


def holders(tile_of_ref, holder):
    n_ctx = tile_of_ref.shape[0]
    for ctx in range(n_ctx):
        holder[tile_of_ref[ctx]] = ctx


def route_kernel(window, place_ref, tile_of_ref, held_ref, out_ref, holder):
    group, n_head = out_ref.shape[:2]
    holders(tile_of_ref, holder)
    first = lax.div(place_ref[0], group) * group

    def one(member, carry):
        for slot in range(window):
            tile = tile_of_ref[first + member] - (window - slot)
            source = holder[jnp.maximum(tile, 0)]
            rows = held_ref[source]
            for head in range(n_head):
                out_ref[member, head, slot] = rows
        return carry

    lax.fori_loop(0, group, one, 0)


def sum_kernel(window, group, place_ref, tile_of_ref, terms_ref, order_ref, out_ref, holder):
    n_ctx, n_head = out_ref.shape[:2]
    holders(tile_of_ref, holder)
    first = lax.div(place_ref[0], group) * group

    def one(ctx, carry):
        total = jnp.zeros(out_ref.shape[2:], F32)
        for slot in range(window):
            tile = tile_of_ref[ctx] + (window - slot)
            source = holder[jnp.minimum(tile, n_ctx - 1)] - first
            here = (tile < n_ctx) & (source >= 0) & (source < group)
            source = jnp.where(here, source, 0)
            part = terms_ref[source, 0, slot].astype(F32)
            for head in range(1, n_head):
                part = part + terms_ref[source, head, slot].astype(F32)
            total = total + jnp.where(here, part, 0.0)
        for head in range(n_head):
            out_ref[ctx, head] = total.astype(BF16)
        return carry

    lax.fori_loop(0, n_ctx, one, 0)


def shape_of(shape, dtype):
    return jax.ShapeDtypeStruct(shape, dtype)


def call(body, name, scalars, arrays, out_shape, scratch, flops, space=VMEM):
    return pl.pallas_call(
        body,
        in_specs=[SMEM] * scalars + [space] * arrays,
        out_specs=(space,) * len(out_shape),
        out_shape=out_shape,
        scratch_shapes=scratch,
        compiler_params=pltpu.CompilerParams(vmem_limit_bytes=VMEM_LIMIT),
        cost_estimate=pl.CostEstimate(
            flops=flops, bytes_accessed=1 << 22, transcendentals=0
        ),
        name=name,
    )


def past_call(window, heads, pieces_shape, row_total, work):
    n_owners, _, _, piece, width = pieces_shape
    past_rows = window * n_owners * piece
    chunks = row_total // ROW_BLOCK
    rows = pltpu.VMEM((row_total, width), BF16)
    stats = pltpu.VMEM((8, row_total), F32)
    win = pltpu.VMEM((2, window, n_owners, piece, width), BF16)
    acc = pltpu.VMEM((past_rows, width), F32)
    dma = pltpu.SemaphoreType.DMA
    return call(
        functools.partial(past_kernel, window, heads),
        "past",
        3,
        4,
        (shape_of((8, row_total), F32), shape_of(pieces_shape, BF16)),
        [
            rows,
            rows,
            stats,
            stats,
            win,
            win,
            acc,
            acc,
            dma((chunks, 2)),
            dma((2, window)),
            dma((2,)),
            dma((2, window)),
        ],
        4 * window * work,
        HBM,
    )


def late_call(window, heads, pieces_shape, row_total, work):
    n_owners, _, _, piece, width = pieces_shape
    chunks = row_total // ROW_BLOCK
    rows = pltpu.VMEM((row_total, width), BF16)
    columns = pltpu.VMEM((width, row_total), BF16)
    dma = pltpu.SemaphoreType.DMA
    return call(
        functools.partial(late_kernel, window, heads),
        "late",
        3,
        7,
        (shape_of((row_total, width), BF16), shape_of((row_total, width), BF16)),
        [
            rows,
            rows,
            pltpu.VMEM((8, row_total), F32),
            pltpu.VMEM((2, window, n_owners, piece, width), BF16),
            columns,
            columns,
            rows,
            rows,
            dma((chunks, 4)),
            dma((2, window)),
            dma((1,)),
            dma((chunks, 2)),
        ],
        4 * window * work,
        HBM,
    )


def own_forward_call(heads, tile_rows, width, row_total, work):
    chunk_pos = ROW_BLOCK // heads
    ends = range(chunk_pos, tile_rows + 1, chunk_pos)
    return call(
        functools.partial(own_forward_kernel, heads),
        "own_forward",
        3,
        4,
        (shape_of((8, row_total), F32),) + tuple(shape_of((end, ROW_BLOCK), BF16) for end in ends),
        [],
        2 * work,
    )


def own_grads_call(heads, tile_rows, width, row_total, work):
    return call(
        functools.partial(own_grads_kernel, heads),
        "own_grads",
        0,
        5 + row_total // ROW_BLOCK,
        (
            shape_of((width, row_total), BF16),
            shape_of((width, row_total), BF16),
            shape_of((2, tile_rows, width), BF16),
        ),
        [pltpu.VMEM((tile_rows, width), F32), pltpu.VMEM((tile_rows, width), F32)],
        4 * work,
    )


def small_call(body, name, out_shape, n_ctx, ordered=0):
    return pl.pallas_call(
        body,
        in_specs=[SMEM, SMEM, VMEM] + [HBM] * ordered,
        out_specs=VMEM,
        out_shape=out_shape,
        scratch_shapes=[pltpu.SMEM((n_ctx,), jnp.int32)],
        compiler_params=pltpu.CompilerParams(vmem_limit_bytes=SMALL_LIMIT),
        name=name,
    )


def on_device(queries, keys, values, grad_out, lengths, tile_of):
    tile_rows, heads, width = queries.shape
    n_ctx = lax.axis_size("ctx")
    n_head = lax.axis_size("head")
    group = n_ctx // 2
    n_owners = group * n_head
    piece = tile_rows // n_owners
    both = ("ctx", "head")
    halves = [list(range(n_owners)), list(range(n_owners, 2 * n_owners))]
    most_doc = n_ctx * tile_rows // 8
    window = -(-(most_doc - 1) // tile_rows)
    row_total = tile_rows * heads
    place = lax.axis_index("ctx").astype(jnp.int32).reshape(1)
    y = lax.axis_index("head")
    scalars = (place, lengths, tile_of)
    q_rows = queries.reshape(row_total, width)
    g_rows = grad_out.reshape(row_total, width)
    work = 2 * row_total * tile_rows * width
    fine = piece % 16 == 0

    pieces = jnp.stack(
        [tile.reshape(group, n_head, piece, width) for tile in (keys, values)], axis=2
    )
    mine = lax.dynamic_index_in_dim(pieces, y, 1, keepdims=False)
    held = lax.all_to_all(jnp.concatenate([mine, mine]), "ctx", 0, 0, tiled=True)
    packed = small_call(
        functools.partial(route_kernel, window),
        "route",
        shape_of((group, n_head, window, 2, piece, width), BF16),
        n_ctx,
    )(place, tile_of, held)
    past = lax.all_to_all(
        packed.reshape(n_owners, window, 2, piece, width),
        both,
        0,
        0,
        tiled=True,
        axis_index_groups=halves,
    )
    pieces_shape = (n_owners, window, 2, piece, width)
    if not fine:
        pieces_shape = (1, window, 2, tile_rows, width)
        past = past.transpose(1, 2, 0, 3, 4).reshape(pieces_shape)

    own_stats, *own_weights = own_forward_call(heads, tile_rows, width, row_total, work)(
        *scalars, q_rows, g_rows, keys, values
    )
    stats, terms = past_call(window, heads, pieces_shape, row_total, work)(
        *scalars, q_rows, g_rows, own_stats, past
    )
    own_out, own_dq, own_grads = own_grads_call(heads, tile_rows, width, row_total, work)(
        q_rows, g_rows, stats, keys, values, *own_weights
    )

    if not fine:
        terms = terms.reshape(window, 2, n_owners, piece, width).transpose(2, 0, 1, 3, 4)
    terms = lax.all_to_all(terms, both, 0, 0, tiled=True, axis_index_groups=halves)
    summed = small_call(
        functools.partial(sum_kernel, window, group),
        "sum_terms",
        shape_of((n_ctx, n_head, 2, piece, width), BF16),
        n_ctx,
        1,
    )(place, tile_of, terms.reshape(group, n_head, window, 2, piece, width), own_grads)
    summed = summed.reshape(n_ctx * n_head, 2, piece, width)
    far = lax.all_to_all(summed, both, 0, 0, tiled=True)
    attended, query_grad = late_call(window, heads, pieces_shape, row_total, work)(
        *scalars, q_rows, g_rows, stats, past, own_out, own_dq, summed
    )

    if n_head == 2:
        peer = lax.ppermute(own_grads, "head", [(0, 1), (1, 0)])
        peer, far, attended = lax.optimization_barrier((peer, far, attended))
        near = own_grads.astype(F32) + peer.astype(F32)
    else:
        near = lax.psum(own_grads.astype(F32), "head")
    far = far.reshape(2, n_owners, 2, piece, width).astype(F32)
    far = far[0] + far[1]
    far_keys, far_values = (far[:, part].reshape(tile_rows, width) for part in range(2))
    return (
        attended.reshape(tile_rows, heads, width),
        query_grad.reshape(tile_rows, heads, width),
        near[0] + far_keys,
        near[1] + far_values,
    )


def solution(mesh):
    return jax.shard_map(
        on_device,
        mesh=mesh,
        in_specs=(
            P("ctx", "head", None),
            P("ctx", None),
            P("ctx", None),
            P("ctx", "head", None),
            P(),
            P(),
        ),
        out_specs=(P("ctx", "head", None), P("ctx", "head", None), P("ctx", None), P("ctx", None)),
        check_vma=False,
    )
```

```python
import functools

import jax
import jax.numpy as jnp
from jax import lax
from jax.experimental import pallas as pl
from jax.experimental.pallas import tpu as pltpu
from jax.sharding import PartitionSpec as P

LOG2E = 1.4426950408889634
NEG_FILL = -1e30
KEY_BLOCK = 256
ROW_BLOCK = 1024
VMEM_LIMIT = 60 * 1024 * 1024
SMALL_LIMIT = 16 * 1024 * 1024
PAST_LIMIT = 52 * 1024 * 1024
STATS_SIZE = 1 << 22
SMEM = pl.BlockSpec(memory_space=pltpu.SMEM)
VMEM = pl.BlockSpec(memory_space=pltpu.VMEM)
ANY = pl.BlockSpec(memory_space=pl.ANY)
HBM = pl.BlockSpec(memory_space=pltpu.HBM)
F32 = jnp.float32
BF16 = jnp.bfloat16


def matmul(left, right):
    return lax.dot_general(left, right, (((1,), (0,)), ((), ())), preferred_element_type=F32)


def matmul_first(left, right):
    return lax.dot_general(left, right, (((0,), (0,)), ((), ())), preferred_element_type=F32)


def matmul_last(left, right):
    return lax.dot_general(left, right, (((1,), (1,)), ((), ())), preferred_element_type=F32)


def fold_rows(block, combine):
    folded = block[0:8]
    for begin in range(8, block.shape[0], 8):
        folded = combine(folded, block[begin : begin + 8])
    return folded


def document_starts(ends, positions):
    start = jnp.zeros_like(positions)
    for end in ends:
        start = jnp.where(end <= positions, end, start)
    return start


def document_ends(lengths_ref):
    ends = []
    total = jnp.int32(0)
    for doc in range(lengths_ref.shape[0]):
        total = total + lengths_ref[doc]
        ends.append(total)
    return ends


def lane_positions(heads, first_pos):
    lane = lax.broadcasted_iota(jnp.int32, (1, ROW_BLOCK), 1)
    return first_pos + lax.div(lane, heads)


def key_positions(keys):
    shape = (keys.stop - keys.start, ROW_BLOCK)
    return keys.start + lax.broadcasted_iota(jnp.int32, shape, 0)


def fold_all(blocks, combine):
    folded = fold_rows(blocks[0], combine)
    for block in blocks[1:]:
        folded = combine(folded, fold_rows(block, combine))
    return folded


def row_blocks(total):
    return [slice(begin, begin + ROW_BLOCK) for begin in range(0, total, ROW_BLOCK)]


def key_blocks(begin, end):
    starts = list(range(end - KEY_BLOCK, begin, -KEY_BLOCK))[::-1]
    starts = [begin] + [start for start in starts if start > begin]
    return [slice(start, stop) for start, stop in zip(starts, starts[1:] + [end])]


def own_forward_kernel(
    heads, place_ref, lengths_ref, tile_of_ref, q_ref, g_ref, k_ref, v_ref, stats_hbm, *refs
):
    *weight_refs, stats_ref, stats_sem = refs
    tile_rows, width = k_ref.shape
    exponent_scale = float(width) ** (-0.5) * LOG2E
    chunk_pos = ROW_BLOCK // heads
    tile_begin = tile_of_ref[place_ref[0]] * tile_rows
    ends = document_ends(lengths_ref)

    for chunk, rows in enumerate(row_blocks(q_ref.shape[0])):
        first_pos = tile_begin + chunk * chunk_pos
        q_pos = lane_positions(heads, first_pos)
        low = document_starts(ends, q_pos) - tile_begin
        high = q_pos - tile_begin
        blocks = key_blocks(0, (chunk + 1) * chunk_pos)
        scores = []
        for keys in blocks:
            score = matmul_last(k_ref[keys, :], q_ref[rows, :])
            key_pos = key_positions(keys)
            live = key_pos >= low
            if keys.stop > chunk * chunk_pos:
                live = live & (key_pos <= high)
            scores.append(jnp.where(live, score, NEG_FILL))
        top = jnp.max(fold_all(scores, jnp.maximum), axis=0, keepdims=True) * exponent_scale
        sums = jnp.zeros((8, ROW_BLOCK), F32)
        products = jnp.zeros((8, ROW_BLOCK), F32)
        for keys, score in zip(blocks, scores):
            weight = jnp.exp2(score * exponent_scale - top)
            weight_refs[chunk][keys, :] = weight.astype(BF16)
            dprob = matmul_last(v_ref[keys, :], g_ref[rows, :])
            sums += fold_rows(weight, jnp.add)
            products += fold_rows(weight * dprob, jnp.add)
        stats_ref[0:1, rows] = top
        stats_ref[1:2, rows] = jnp.sum(sums, axis=0, keepdims=True)
        stats_ref[2:3, rows] = jnp.sum(products, axis=0, keepdims=True)

    first_start, first_end = crossing(ends, tile_begin)
    for row, value in ((3, tile_begin), (4, first_start), (5, first_end)):
        stats_ref[row : row + 1, :] = jnp.full((1, stats_ref.shape[1]), value, jnp.int32).astype(F32)
    stats_out = pltpu.make_async_copy(stats_ref, stats_hbm.at[0:8], stats_sem.at[0])
    stats_out.start()
    stats_out.wait()


def crossing(ends, tile_begin):
    first_start, first_end = jnp.int32(0), jnp.int32(0)
    for end in ends:
        crosses = (first_end <= tile_begin) & (end > tile_begin)
        first_start = jnp.where(end <= tile_begin, end, first_start)
        first_end = jnp.where(crosses, end, first_end)
    return first_start, first_end


class Past:
    def __init__(self, window, heads, past_hbm, win_ref):
        _, _, n_owners, self.piece, self.width = win_ref.shape
        self.n_owners = n_owners
        self.tile_rows = n_owners * self.piece
        self.past_rows = window * self.tile_rows
        self.chunk_pos = ROW_BLOCK // heads
        self.heads = heads
        self.window = window
        self.past_hbm = past_hbm
        self.win_ref = win_ref
        self.unit = window * KEY_BLOCK // 4
        self.branches = self.past_rows // self.unit

    def plan(self, stats_ref):
        plan = [jnp.max(stats_ref[row : row + 1, 0:128]).astype(jnp.int32) for row in (3, 4, 5)]
        self.tile_begin, first_start, self.first_end = plan
        self.first_key = jnp.maximum(self.past_rows - (self.tile_begin - first_start), 0)
        self.all_units = self.branches - lax.div(self.first_key, self.unit)

    def copies(self, part, sem):
        return [
            pltpu.make_async_copy(
                self.past_hbm.at[:, slot, part],
                self.win_ref.at[part, slot],
                sem.at[part, slot],
            )
            for slot in range(self.window)
        ]

    def rows(self, part, keys):
        slot, begin = divmod(keys.start, self.tile_rows)
        end = begin + keys.stop - keys.start
        if end > self.tile_rows:
            border = (slot + 1) * self.tile_rows
            parts = [
                self.rows(part, slice(keys.start, border)),
                self.rows(part, slice(border, keys.stop)),
            ]
            return jnp.concatenate(parts, axis=0)
        if self.n_owners == 1:
            return self.win_ref[part, slot, 0, begin:end, :]
        rows = self.win_ref[part, slot, begin // self.piece : end // self.piece]
        return rows.reshape(end - begin, self.width)

    def scores(self, units, q_rows):
        blocks = key_blocks(self.past_rows - units * self.unit, self.past_rows)
        scores = [matmul_last(self.rows(0, keys), q_rows) for keys in blocks]
        live = key_positions(blocks[0]) >= self.first_key
        scores[0] = jnp.where(live, scores[0], NEG_FILL)
        return blocks, scores

    def by_units(self, chunk, nothing, branch):
        first_pos = self.tile_begin + chunk * self.chunk_pos
        live_units = jnp.where(first_pos < self.first_end, self.all_units, 0)
        pl.when(live_units == 0)(nothing)
        for units in range(1, self.branches + 1):
            pl.when(live_units == units)(functools.partial(branch, units))

    def has_past(self, chunk):
        first_pos = self.tile_begin + chunk * self.chunk_pos
        return lane_positions(self.heads, first_pos) < self.first_end


def chunk_rows(chunk):
    return pl.ds(pl.multiple_of(chunk * ROW_BLOCK, ROW_BLOCK), ROW_BLOCK)


def chunk_copies(pairs, sem, chunk):
    rows = chunk_rows(chunk)
    copies = []
    for index, (source, target, axis) in enumerate(pairs):
        where = (rows, slice(None)) if axis == 0 else (slice(None), rows)
        copies.append(
            pltpu.make_async_copy(source.at[where], target.at[where], sem.at[chunk, index])
        )
    return copies


def start_all(copies):
    for copy in copies:
        copy.start()


def wait_all(copies):
    for copy in copies:
        copy.wait()


def past_kernel(
    window,
    heads,
    q_hbm,
    g_hbm,
    own_stats_hbm,
    past_hbm,
    kept_in_hbm,
    stats_hbm,
    terms_hbm,
    kept_hbm,
    q_ref,
    g_ref,
    own_stats_ref,
    stats_ref,
    win_ref,
    terms_ref,
    dk_acc,
    dv_acc,
    in_sem,
    past_sem,
    stats_sem,
    terms_sem,
    kept_sem,
):
    past = Past(window, heads, past_hbm, win_ref)
    past_rows, width = dk_acc.shape
    scale = float(width) ** (-0.5)
    exponent_scale = scale * LOG2E
    chunks = q_ref.shape[0] // ROW_BLOCK
    pairs = ((q_hbm, q_ref, 0), (g_hbm, g_ref, 0))
    stats_in = pltpu.make_async_copy(own_stats_hbm.at[0:8], own_stats_ref, stats_sem.at[0])
    stats_out = pltpu.make_async_copy(stats_ref, stats_hbm.at[0:8], stats_sem.at[1])

    start_all(past.copies(0, past_sem))
    start_all(chunk_copies(pairs, in_sem, 0))
    stats_in.start()
    start_all(past.copies(1, past_sem))
    for chunk in range(1, chunks):
        start_all(chunk_copies(pairs, in_sem, chunk))
    dk_acc[...] = jnp.zeros_like(dk_acc)
    dv_acc[...] = jnp.zeros_like(dv_acc)
    wait_all(past.copies(0, past_sem) + past.copies(1, past_sem) + [stats_in])
    past.plan(own_stats_ref)
    stats_ref[3:6, :] = own_stats_ref[3:6, :]
    keep = [
        pltpu.make_async_copy(
            win_ref.at[part, slot], kept_hbm.at[:, slot, part], kept_sem.at[part, slot]
        )
        for part in range(2)
        for slot in range(window)
    ]
    start_all(keep)

    def chunk_step(chunk, carry):
        rows = chunk_rows(chunk)
        wait_all(chunk_copies(pairs, in_sem, chunk))
        own_top = own_stats_ref[0:1, rows]
        own_sum = own_stats_ref[1:2, rows]
        own_product = own_stats_ref[2:3, rows]

        def branch(units):
            has_past = past.has_past(chunk)
            q_rows = q_ref[rows, :]
            g_rows = g_ref[rows, :]
            blocks, scores = past.scores(units, q_rows)
            dprobs = [matmul_last(past.rows(1, keys), g_rows) for keys in blocks]
            top = jnp.max(fold_all(scores, jnp.maximum), axis=0, keepdims=True)
            top = jnp.where(has_past, jnp.maximum(top * exponent_scale, own_top), own_top)
            shift = jnp.where(has_past, top, -NEG_FILL)
            sums = jnp.zeros((8, ROW_BLOCK), F32)
            products = jnp.zeros((8, ROW_BLOCK), F32)
            weights = []
            for score, dprob in zip(scores, dprobs):
                weight = jnp.exp2(score * exponent_scale - shift)
                sums += fold_rows(weight, jnp.add)
                products += fold_rows(weight * dprob, jnp.add)
                weights.append(weight.astype(BF16))
            rescale = jnp.exp2(own_top - top)
            total = own_sum * rescale + jnp.sum(sums, axis=0, keepdims=True)
            product = own_product * rescale + jnp.sum(products, axis=0, keepdims=True)
            inverse = 1.0 / total
            delta = product * inverse
            stats_ref[0:1, rows] = rescale * inverse
            stats_ref[1:2, rows] = delta
            stats_ref[2:3, rows] = jnp.where(has_past, top + jnp.log2(total), -NEG_FILL)
            inverse_low = inverse.astype(BF16)
            probs = [weight * inverse_low for weight in weights]
            for keys, prob in zip(blocks, probs):
                dv_acc[keys, :] += matmul(prob, g_rows)
            for keys, prob, dprob in zip(blocks, probs, dprobs):
                dscore = prob * (dprob - delta).astype(BF16)
                dk_acc[keys, :] += matmul(dscore, q_rows)

        def nothing():
            inverse = 1.0 / own_sum
            stats_ref[0:1, rows] = inverse
            stats_ref[1:2, rows] = own_product * inverse
            stats_ref[2:3, rows] = jnp.full((1, ROW_BLOCK), -NEG_FILL, F32)

        past.by_units(chunk, nothing, branch)
        return carry

    lax.fori_loop(0, chunks, chunk_step, 0)
    stats_out.start()
    copies = [stats_out] + keep
    for slot in range(window):
        rows = slice(slot * past.tile_rows, (slot + 1) * past.tile_rows)
        shape = (past.n_owners, past.piece, width)
        terms_ref[0, slot] = (dk_acc[rows, :] * scale).astype(BF16).reshape(shape)
        terms_ref[1, slot] = dv_acc[rows, :].astype(BF16).reshape(shape)
        for part in range(2):
            copy = pltpu.make_async_copy(
                terms_ref.at[part, slot], terms_hbm.at[:, slot, part], terms_sem.at[part, slot]
            )
            copy.start()
            copies.append(copy)
    wait_all(copies)


def late_kernel(
    window,
    heads,
    q_hbm,
    g_hbm,
    stats_hbm,
    past_hbm,
    own_out_hbm,
    own_dq_hbm,
    summed_hbm,
    att_hbm,
    dq_hbm,
    q_ref,
    g_ref,
    stats_ref,
    win_ref,
    own_out_ref,
    own_dq_ref,
    att_ref,
    dq_ref,
    in_sem,
    past_sem,
    stats_sem,
    out_sem,
):
    past = Past(window, heads, past_hbm, win_ref)
    width = past.width
    scale = float(width) ** (-0.5)
    exponent_scale = scale * LOG2E
    chunks = q_ref.shape[0] // ROW_BLOCK
    pairs = (
        (q_hbm, q_ref, 0),
        (g_hbm, g_ref, 0),
        (own_out_hbm, own_out_ref, 1),
        (own_dq_hbm, own_dq_ref, 1),
    )
    out_pairs = ((att_ref, att_hbm, 0), (dq_ref, dq_hbm, 0))
    stats_in = pltpu.make_async_copy(stats_hbm.at[0:8], stats_ref, stats_sem.at[0])
    window_in = past.copies(0, past_sem) + past.copies(1, past_sem) + [stats_in]
    start_all(window_in)
    for chunk in range(chunks):
        start_all(chunk_copies(pairs, in_sem, chunk))
    wait_all(window_in)
    past.plan(stats_ref)

    def chunk_step(chunk, carry):
        rows = chunk_rows(chunk)
        wait_all(chunk_copies(pairs, in_sem, chunk))

        def branch(units):
            q_rows = q_ref[rows, :]
            g_rows = g_ref[rows, :]
            delta = stats_ref[1:2, rows]
            shift = stats_ref[2:3, rows]
            blocks, scores = past.scores(units, q_rows)
            out_turned = own_out_ref[:, rows].astype(F32)
            dq_turned = own_dq_ref[:, rows].astype(F32)
            for keys, score in zip(blocks, scores):
                prob = jnp.exp2(score * exponent_scale - shift).astype(BF16)
                out_turned += matmul_first(past.rows(1, keys), prob)
                dprob = matmul_last(past.rows(1, keys), g_rows)
                dscore = prob * (dprob - delta).astype(BF16)
                dq_turned += matmul_first(past.rows(0, keys), dscore)
            att_ref[rows, :] = out_turned.astype(BF16).T
            dq_ref[rows, :] = (dq_turned * scale).astype(BF16).T

        def nothing():
            att_ref[rows, :] = own_out_ref[:, rows].T
            dq_ref[rows, :] = (own_dq_ref[:, rows].astype(F32) * scale).astype(BF16).T

        past.by_units(chunk, nothing, branch)
        start_all(chunk_copies(out_pairs, out_sem, chunk))
        return carry

    lax.fori_loop(0, chunks, chunk_step, 0)
    for chunk in range(chunks):
        wait_all(chunk_copies(out_pairs, out_sem, chunk))


def own_grads_kernel(
    heads, q_ref, g_ref, stats_hbm, k_ref, v_ref, *refs
):
    tile_rows, width = k_ref.shape
    chunk_pos = ROW_BLOCK // heads
    chunks = q_ref.shape[0] // ROW_BLOCK
    weight_refs = refs[:chunks]
    out_ref, dq_ref, dkv_ref, stats_ref, stats_sem, dk_acc, dv_acc = refs[chunks:]
    scale = float(width) ** (-0.5)
    stats_in = pltpu.make_async_copy(stats_hbm.at[0:8], stats_ref, stats_sem.at[0])
    stats_in.start()
    dk_acc[...] = jnp.zeros_like(dk_acc)
    dv_acc[...] = jnp.zeros_like(dv_acc)
    stats_in.wait()

    for chunk, rows in enumerate(row_blocks(q_ref.shape[0])):
        rescale = stats_ref[0:1, rows]
        delta = stats_ref[1:2, rows]
        q_rows = q_ref[rows, :]
        g_rows = g_ref[rows, :]
        out_turned = jnp.zeros((width, ROW_BLOCK), F32)
        dq_turned = jnp.zeros((width, ROW_BLOCK), F32)
        for keys in key_blocks(0, (chunk + 1) * chunk_pos):
            prob = (weight_refs[chunk][keys, :].astype(F32) * rescale).astype(BF16)
            dprob = matmul_last(v_ref[keys, :], g_rows)
            dscore = prob * (dprob - delta).astype(BF16)
            dv_acc[keys, :] += matmul(prob, g_rows)
            dk_acc[keys, :] += matmul(dscore, q_rows)
            out_turned += matmul_first(v_ref[keys, :], prob)
            dq_turned += matmul_first(k_ref[keys, :], dscore)
        out_ref[:, rows] = out_turned.astype(BF16)
        dq_ref[:, rows] = dq_turned.astype(BF16)

    dkv_ref[0] = (dk_acc[...] * scale).astype(BF16)
    dkv_ref[1] = dv_acc[...].astype(BF16)


def holders(tile_of_ref, holder):
    n_ctx = tile_of_ref.shape[0]
    for ctx in range(n_ctx):
        holder[tile_of_ref[ctx]] = ctx


def route_kernel(window, place_ref, tile_of_ref, held_hbm, out_hbm, holder, sem):
    group, n_head = out_hbm.shape[:2]
    holders(tile_of_ref, holder)
    first = lax.div(place_ref[0], group) * group
    for member in range(group):
        for slot in range(window):
            tile = tile_of_ref[first + member] - (window - slot)
            source = holder[jnp.maximum(tile, 0)]
            for head in range(n_head):
                pltpu.make_async_copy(
                    held_hbm.at[source], out_hbm.at[member, head, slot], sem.at[member]
                ).start()
    for member in range(group):
        whole = out_hbm.at[member]
        pltpu.make_async_copy(whole, whole, sem.at[member]).wait()


def sum_kernel(window, group, place_ref, tile_of_ref, terms_ref, out_hbm, holder, summed, sem):
    n_ctx, n_head = out_hbm.shape[:2]
    holders(tile_of_ref, holder)
    first = lax.div(place_ref[0], group) * group

    def one(ctx, carry):
        total = jnp.zeros(summed.shape[1:], F32)
        for slot in range(window):
            tile = tile_of_ref[ctx] + (window - slot)
            source = holder[jnp.minimum(tile, n_ctx - 1)] - first
            here = (tile < n_ctx) & (source >= 0) & (source < group)
            source = jnp.where(here, source, 0)
            part = terms_ref[source, 0, slot].astype(F32)
            for head in range(1, n_head):
                part = part + terms_ref[source, head, slot].astype(F32)
            total = total + jnp.where(here, part, 0.0)
        summed[ctx] = total.astype(BF16)
        for head in range(n_head):
            pltpu.make_async_copy(summed.at[ctx], out_hbm.at[ctx, head], sem.at[head]).start()
        return carry

    lax.fori_loop(0, n_ctx, one, 0)
    for head in range(n_head):
        pltpu.make_async_copy(summed, out_hbm.at[:, head], sem.at[head]).wait()


def shape_of(shape, dtype):
    return jax.ShapeDtypeStruct(shape, dtype)


def call(body, name, specs, out_shape, scratch, flops, space=VMEM, limit=VMEM_LIMIT, aliases=()):
    return pl.pallas_call(
        body,
        in_specs=specs,
        out_specs=space if isinstance(space, list) else [space] * len(out_shape),
        out_shape=out_shape,
        scratch_shapes=scratch,
        compiler_params=pltpu.CompilerParams(vmem_limit_bytes=limit),
        cost_estimate=pl.CostEstimate(
            flops=flops, bytes_accessed=1 << 22, transcendentals=0
        ),
        input_output_aliases=dict(aliases),
        name=name,
    )


def stats_shape(row_total):
    return shape_of((STATS_SIZE // row_total, row_total), F32)


def past_call(window, heads, pieces_shape, row_total, work):
    n_owners, _, _, piece, width = pieces_shape
    past_rows = window * n_owners * piece
    chunks = row_total // ROW_BLOCK
    rows = pltpu.VMEM((row_total, width), BF16)
    stats = pltpu.VMEM((8, row_total), F32)
    win = pltpu.VMEM((2, window, n_owners, piece, width), BF16)
    acc = pltpu.VMEM((past_rows, width), F32)
    dma = pltpu.SemaphoreType.DMA
    return call(
        functools.partial(past_kernel, window, heads),
        "past",
        [HBM] * 3 + [ANY, HBM],
        (
            stats_shape(row_total),
            shape_of(pieces_shape, BF16),
            shape_of(pieces_shape, BF16),
        ),
        [
            rows,
            rows,
            stats,
            stats,
            win,
            win,
            acc,
            acc,
            dma((chunks, 2)),
            dma((2, window)),
            dma((2,)),
            dma((2, window)),
            dma((2, window)),
        ],
        4 * window * work,
        HBM,
        PAST_LIMIT,
        ((4, 2),),
    )


def late_call(window, heads, pieces_shape, row_total, work):
    n_owners, _, _, piece, width = pieces_shape
    chunks = row_total // ROW_BLOCK
    rows = pltpu.VMEM((row_total, width), BF16)
    columns = pltpu.VMEM((width, row_total), BF16)
    dma = pltpu.SemaphoreType.DMA
    return call(
        functools.partial(late_kernel, window, heads),
        "late",
        [HBM] * 7,
        (shape_of((row_total, width), BF16), shape_of((row_total, width), BF16)),
        [
            rows,
            rows,
            pltpu.VMEM((8, row_total), F32),
            pltpu.VMEM((2, window, n_owners, piece, width), BF16),
            columns,
            columns,
            rows,
            rows,
            dma((chunks, 4)),
            dma((2, window)),
            dma((1,)),
            dma((chunks, 2)),
        ],
        4 * window * work,
        HBM,
    )


def own_forward_call(heads, tile_rows, width, row_total, work):
    chunk_pos = ROW_BLOCK // heads
    ends = range(chunk_pos, tile_rows + 1, chunk_pos)
    return call(
        functools.partial(own_forward_kernel, heads),
        "own_forward",
        [SMEM] * 3 + [VMEM] * 4,
        (stats_shape(row_total),) + tuple(shape_of((end, ROW_BLOCK), BF16) for end in ends),
        [pltpu.VMEM((8, row_total), F32), pltpu.SemaphoreType.DMA((1,))],
        2 * work,
        [HBM] + [VMEM] * len(ends),
    )


def own_grads_call(heads, tile_rows, width, row_total, work):
    return call(
        functools.partial(own_grads_kernel, heads),
        "own_grads",
        [VMEM] * 2 + [HBM] + [VMEM] * (2 + row_total // ROW_BLOCK),
        (
            shape_of((width, row_total), BF16),
            shape_of((width, row_total), BF16),
            shape_of((2, tile_rows, width), BF16),
        ),
        [
            pltpu.VMEM((8, row_total), F32),
            pltpu.SemaphoreType.DMA((1,)),
            pltpu.VMEM((tile_rows, width), F32),
            pltpu.VMEM((tile_rows, width), F32),
        ],
        4 * work,
    )


def small_call(body, name, scalars, specs, out_shape, scratch):
    return pl.pallas_call(
        body,
        in_specs=[SMEM] * scalars + specs,
        out_specs=HBM,
        out_shape=out_shape,
        scratch_shapes=scratch,
        compiler_params=pltpu.CompilerParams(vmem_limit_bytes=SMALL_LIMIT),
        name=name,
    )


def on_device(queries, keys, values, grad_out, lengths, tile_of):
    tile_rows, heads, width = queries.shape
    n_ctx = lax.axis_size("ctx")
    n_head = lax.axis_size("head")
    group = n_ctx // 2
    n_owners = group * n_head
    piece = tile_rows // n_owners
    both = ("ctx", "head")
    halves = [list(range(n_owners)), list(range(n_owners, 2 * n_owners))]
    most_doc = n_ctx * tile_rows // 8
    window = -(-(most_doc - 1) // tile_rows)
    row_total = tile_rows * heads
    place = lax.axis_index("ctx").astype(jnp.int32).reshape(1)
    y = lax.axis_index("head")
    scalars = (place, lengths, tile_of)
    q_rows = queries.reshape(row_total, width)
    g_rows = grad_out.reshape(row_total, width)
    work = 2 * row_total * tile_rows * width
    fine = piece % 16 == 0

    shape = (2, group, 1, piece, width)
    mine = [
        lax.dynamic_index_in_dim(tile.reshape(group, n_head, piece, width), y, 1)
        for tile in (keys, values)
    ]
    mine = jnp.concatenate([jnp.broadcast_to(part[None], shape) for part in mine], axis=2)
    held = lax.all_to_all(
        mine.reshape(n_ctx, 2, piece, width), "ctx", 0, 0, tiled=True
    )
    packed = small_call(
        functools.partial(route_kernel, window),
        "route",
        2,
        [ANY],
        shape_of((group, n_head, window, 2, piece, width), BF16),
        [pltpu.SMEM((n_ctx,), jnp.int32), pltpu.SemaphoreType.DMA((group,))],
    )(place, tile_of, held)
    past = lax.all_to_all(
        packed.reshape(n_owners, window, 2, piece, width),
        both,
        0,
        0,
        tiled=True,
        axis_index_groups=halves,
    )
    pieces_shape = (n_owners, window, 2, piece, width)
    if not fine:
        pieces_shape = (1, window, 2, tile_rows, width)
        past = past.transpose(1, 2, 0, 3, 4).reshape(pieces_shape)

    own_stats, *own_weights = own_forward_call(heads, tile_rows, width, row_total, work)(
        *scalars, q_rows, g_rows, keys, values
    )
    stats, terms, kept = past_call(window, heads, pieces_shape, row_total, work)(
        q_rows, g_rows, own_stats, past, packed.reshape(pieces_shape)
    )
    own_out, own_dq, own_grads = own_grads_call(heads, tile_rows, width, row_total, work)(
        q_rows, g_rows, stats, keys, values, *own_weights
    )

    if not fine:
        terms = terms.reshape(window, 2, n_owners, piece, width).transpose(2, 0, 1, 3, 4)
    terms = lax.all_to_all(terms, both, 0, 0, tiled=True, axis_index_groups=halves)
    terms, own_grads = lax.optimization_barrier((terms, own_grads))
    summed = small_call(
        functools.partial(sum_kernel, window, group),
        "sum_terms",
        2,
        [VMEM],
        shape_of((n_ctx, n_head, 2, piece, width), BF16),
        [
            pltpu.SMEM((n_ctx,), jnp.int32),
            pltpu.VMEM((n_ctx, 2, piece, width), BF16),
            pltpu.SemaphoreType.DMA((n_head,)),
        ],
    )(place, tile_of, terms.reshape(group, n_head, window, 2, piece, width))
    summed = summed.reshape(n_ctx * n_head, 2, piece, width)
    far = lax.all_to_all(summed, both, 0, 0, tiled=True)
    attended, query_grad = late_call(window, heads, pieces_shape, row_total, work)(
        q_rows, g_rows, stats, kept, own_out, own_dq, summed
    )

    if n_head == 2:
        peer = lax.ppermute(own_grads, "head", [(0, 1), (1, 0)])
        peer, far, attended = lax.optimization_barrier((peer, far, attended))
        near = own_grads.astype(F32) + peer.astype(F32)
    else:
        near = lax.psum(own_grads.astype(F32), "head")
    far = far.reshape(2, n_owners, 2, piece, width).astype(F32)
    far = far[0] + far[1]
    far_keys, far_values = (far[:, part].reshape(tile_rows, width) for part in range(2))
    return (
        attended.reshape(tile_rows, heads, width),
        query_grad.reshape(tile_rows, heads, width),
        near[0] + far_keys,
        near[1] + far_values,
    )


def solution(mesh):
    return jax.shard_map(
        on_device,
        mesh=mesh,
        in_specs=(
            P("ctx", "head", None),
            P("ctx", None),
            P("ctx", None),
            P("ctx", "head", None),
            P(),
            P(),
        ),
        out_specs=(P("ctx", "head", None), P("ctx", "head", None), P("ctx", None), P("ctx", None)),
        check_vma=False,
    )
```

```python
import functools

import jax
import jax.numpy as jnp
from jax import lax
from jax.experimental import pallas as pl
from jax.experimental.pallas import tpu as pltpu
from jax.sharding import PartitionSpec as P

LOG2E = 1.4426950408889634
NEG_FILL = -1e30
KEY_BLOCK = 256
ROW_BLOCK = 1024
VMEM_LIMIT = 60 * 1024 * 1024
SMALL_LIMIT = 16 * 1024 * 1024
PAST_LIMIT = 52 * 1024 * 1024
STATS_SIZE = 1 << 22
SMEM = pl.BlockSpec(memory_space=pltpu.SMEM)
VMEM = pl.BlockSpec(memory_space=pltpu.VMEM)
ANY = pl.BlockSpec(memory_space=pl.ANY)
HBM = pl.BlockSpec(memory_space=pltpu.HBM)
F32 = jnp.float32
BF16 = jnp.bfloat16


def matmul(left, right):
    return lax.dot_general(left, right, (((1,), (0,)), ((), ())), preferred_element_type=F32)


def matmul_first(left, right):
    return lax.dot_general(left, right, (((0,), (0,)), ((), ())), preferred_element_type=F32)


def matmul_last(left, right):
    return lax.dot_general(left, right, (((1,), (1,)), ((), ())), preferred_element_type=F32)


def fold_rows(block, combine):
    folded = block[0:8]
    for begin in range(8, block.shape[0], 8):
        folded = combine(folded, block[begin : begin + 8])
    return folded


def document_starts(ends, positions):
    start = jnp.zeros_like(positions)
    for end in ends:
        start = jnp.where(end <= positions, end, start)
    return start


def document_ends(lengths_ref):
    ends = []
    total = jnp.int32(0)
    for doc in range(lengths_ref.shape[0]):
        total = total + lengths_ref[doc]
        ends.append(total)
    return ends


def lane_positions(heads, first_pos):
    lane = lax.broadcasted_iota(jnp.int32, (1, ROW_BLOCK), 1)
    return first_pos + lax.div(lane, heads)


def key_positions(keys):
    shape = (keys.stop - keys.start, ROW_BLOCK)
    return keys.start + lax.broadcasted_iota(jnp.int32, shape, 0)


def fold_all(blocks, combine):
    folded = fold_rows(blocks[0], combine)
    for block in blocks[1:]:
        folded = combine(folded, fold_rows(block, combine))
    return folded


def row_blocks(total):
    return [slice(begin, begin + ROW_BLOCK) for begin in range(0, total, ROW_BLOCK)]


def key_blocks(begin, end):
    starts = list(range(end - KEY_BLOCK, begin, -KEY_BLOCK))[::-1]
    starts = [begin] + [start for start in starts if start > begin]
    return [slice(start, stop) for start, stop in zip(starts, starts[1:] + [end])]


def own_forward_kernel(
    heads, place_ref, lengths_ref, tile_of_ref, q_ref, g_ref, k_ref, v_ref, stats_hbm, *refs
):
    *weight_refs, stats_ref, stats_sem = refs
    tile_rows, width = k_ref.shape
    exponent_scale = float(width) ** (-0.5) * LOG2E
    chunk_pos = ROW_BLOCK // heads
    tile_begin = tile_of_ref[place_ref[0]] * tile_rows
    ends = document_ends(lengths_ref)

    for chunk, rows in enumerate(row_blocks(q_ref.shape[0])):
        first_pos = tile_begin + chunk * chunk_pos
        q_pos = lane_positions(heads, first_pos)
        low = document_starts(ends, q_pos) - tile_begin
        high = q_pos - tile_begin
        blocks = key_blocks(0, (chunk + 1) * chunk_pos)
        scores = []
        for keys in blocks:
            score = matmul_last(k_ref[keys, :], q_ref[rows, :])
            key_pos = key_positions(keys)
            live = key_pos >= low
            if keys.stop > chunk * chunk_pos:
                live = live & (key_pos <= high)
            scores.append(jnp.where(live, score, NEG_FILL))
        top = jnp.max(fold_all(scores, jnp.maximum), axis=0, keepdims=True) * exponent_scale
        sums = jnp.zeros((8, ROW_BLOCK), F32)
        products = jnp.zeros((8, ROW_BLOCK), F32)
        for keys, score in zip(blocks, scores):
            weight = jnp.exp2(score * exponent_scale - top)
            weight_refs[chunk][keys, :] = weight.astype(BF16)
            dprob = matmul_last(v_ref[keys, :], g_ref[rows, :])
            sums += fold_rows(weight, jnp.add)
            products += fold_rows(weight * dprob, jnp.add)
        stats_ref[0:1, rows] = top
        stats_ref[1:2, rows] = jnp.sum(sums, axis=0, keepdims=True)
        stats_ref[2:3, rows] = jnp.sum(products, axis=0, keepdims=True)

    first_start, first_end = crossing(ends, tile_begin)
    for row, value in ((3, tile_begin), (4, first_start), (5, first_end)):
        stats_ref[row : row + 1, :] = jnp.full((1, stats_ref.shape[1]), value, jnp.int32).astype(F32)
    stats_out = pltpu.make_async_copy(stats_ref, stats_hbm.at[0:8], stats_sem.at[0])
    stats_out.start()
    stats_out.wait()


def crossing(ends, tile_begin):
    first_start, first_end = jnp.int32(0), jnp.int32(0)
    for end in ends:
        crosses = (first_end <= tile_begin) & (end > tile_begin)
        first_start = jnp.where(end <= tile_begin, end, first_start)
        first_end = jnp.where(crosses, end, first_end)
    return first_start, first_end


class Past:
    def __init__(self, window, heads, past_hbm, win_ref):
        _, _, n_owners, self.piece, self.width = win_ref.shape
        self.n_owners = n_owners
        self.tile_rows = n_owners * self.piece
        self.past_rows = window * self.tile_rows
        self.chunk_pos = ROW_BLOCK // heads
        self.heads = heads
        self.window = window
        self.past_hbm = past_hbm
        self.win_ref = win_ref
        self.unit = window * KEY_BLOCK // 4
        self.branches = self.past_rows // self.unit

    def plan(self, stats_ref):
        plan = [jnp.max(stats_ref[row : row + 1, 0:128]).astype(jnp.int32) for row in (3, 4, 5)]
        self.tile_begin, first_start, self.first_end = plan
        self.first_key = jnp.maximum(self.past_rows - (self.tile_begin - first_start), 0)
        self.all_units = self.branches - lax.div(self.first_key, self.unit)

    def copies(self, part, sem):
        return [
            pltpu.make_async_copy(
                self.past_hbm.at[:, slot, part],
                self.win_ref.at[part, slot],
                sem.at[part, slot],
            )
            for slot in range(self.window)
        ]

    def rows(self, part, keys):
        slot, begin = divmod(keys.start, self.tile_rows)
        end = begin + keys.stop - keys.start
        if end > self.tile_rows:
            border = (slot + 1) * self.tile_rows
            parts = [
                self.rows(part, slice(keys.start, border)),
                self.rows(part, slice(border, keys.stop)),
            ]
            return jnp.concatenate(parts, axis=0)
        if self.n_owners == 1:
            return self.win_ref[part, slot, 0, begin:end, :]
        rows = self.win_ref[part, slot, begin // self.piece : end // self.piece]
        return rows.reshape(end - begin, self.width)

    def scores(self, units, q_rows):
        blocks = key_blocks(self.past_rows - units * self.unit, self.past_rows)
        scores = [matmul_last(self.rows(0, keys), q_rows) for keys in blocks]
        live = key_positions(blocks[0]) >= self.first_key
        scores[0] = jnp.where(live, scores[0], NEG_FILL)
        return blocks, scores

    def by_units(self, chunk, nothing, branch):
        first_pos = self.tile_begin + chunk * self.chunk_pos
        live_units = jnp.where(first_pos < self.first_end, self.all_units, 0)
        pl.when(live_units == 0)(nothing)
        for units in range(1, self.branches + 1):
            pl.when(live_units == units)(functools.partial(branch, units))

    def has_past(self, chunk):
        first_pos = self.tile_begin + chunk * self.chunk_pos
        return lane_positions(self.heads, first_pos) < self.first_end


def chunk_rows(chunk):
    return pl.ds(pl.multiple_of(chunk * ROW_BLOCK, ROW_BLOCK), ROW_BLOCK)


def chunk_copies(pairs, sem, chunk):
    rows = chunk_rows(chunk)
    copies = []
    for index, (source, target, axis) in enumerate(pairs):
        where = (rows, slice(None)) if axis == 0 else (slice(None), rows)
        copies.append(
            pltpu.make_async_copy(source.at[where], target.at[where], sem.at[chunk, index])
        )
    return copies


def start_all(copies):
    for copy in copies:
        copy.start()


def wait_all(copies):
    for copy in copies:
        copy.wait()


def past_kernel(
    window,
    heads,
    q_hbm,
    g_hbm,
    own_stats_hbm,
    past_hbm,
    kept_in_hbm,
    stats_hbm,
    terms_hbm,
    kept_hbm,
    q_ref,
    g_ref,
    own_stats_ref,
    stats_ref,
    win_ref,
    terms_ref,
    dk_acc,
    dv_acc,
    in_sem,
    past_sem,
    stats_sem,
    terms_sem,
    kept_sem,
):
    past = Past(window, heads, past_hbm, win_ref)
    past_rows, width = dk_acc.shape
    scale = float(width) ** (-0.5)
    exponent_scale = scale * LOG2E
    chunks = q_ref.shape[0] // ROW_BLOCK
    pairs = ((q_hbm, q_ref, 0), (g_hbm, g_ref, 0))
    stats_in = pltpu.make_async_copy(own_stats_hbm.at[0:8], own_stats_ref, stats_sem.at[0])
    stats_out = pltpu.make_async_copy(stats_ref, stats_hbm.at[0:8], stats_sem.at[1])

    stats_in.start()
    start_all(past.copies(0, past_sem))
    start_all(chunk_copies(pairs, in_sem, 0))
    start_all(past.copies(1, past_sem))
    for chunk in range(1, chunks):
        start_all(chunk_copies(pairs, in_sem, chunk))
    dk_acc[...] = jnp.zeros_like(dk_acc)
    dv_acc[...] = jnp.zeros_like(dv_acc)
    stats_in.wait()
    past.plan(own_stats_ref)
    wait_all(past.copies(0, past_sem) + past.copies(1, past_sem))
    stats_ref[3:6, :] = own_stats_ref[3:6, :]
    keep = [
        pltpu.make_async_copy(
            win_ref.at[part, slot], kept_hbm.at[:, slot, part], kept_sem.at[part, slot]
        )
        for part in range(2)
        for slot in range(window)
    ]
    start_all(keep)

    def chunk_step(chunk, carry):
        rows = chunk_rows(chunk)
        wait_all(chunk_copies(pairs, in_sem, chunk))
        own_top = own_stats_ref[0:1, rows]
        own_sum = own_stats_ref[1:2, rows]
        own_product = own_stats_ref[2:3, rows]

        def branch(units):
            has_past = past.has_past(chunk)
            q_rows = q_ref[rows, :]
            g_rows = g_ref[rows, :]
            blocks, scores = past.scores(units, q_rows)
            dprobs = [matmul_last(past.rows(1, keys), g_rows) for keys in blocks]
            top = jnp.max(fold_all(scores, jnp.maximum), axis=0, keepdims=True)
            top = jnp.where(has_past, jnp.maximum(top * exponent_scale, own_top), own_top)
            shift = jnp.where(has_past, top, -NEG_FILL)
            sums = jnp.zeros((8, ROW_BLOCK), F32)
            products = jnp.zeros((8, ROW_BLOCK), F32)
            weights = []
            for score, dprob in zip(scores, dprobs):
                weight = jnp.exp2(score * exponent_scale - shift)
                sums += fold_rows(weight, jnp.add)
                products += fold_rows(weight * dprob, jnp.add)
                weights.append(weight.astype(BF16))
            rescale = jnp.exp2(own_top - top)
            total = own_sum * rescale + jnp.sum(sums, axis=0, keepdims=True)
            product = own_product * rescale + jnp.sum(products, axis=0, keepdims=True)
            inverse = 1.0 / total
            delta = product * inverse
            stats_ref[0:1, rows] = rescale * inverse
            stats_ref[1:2, rows] = delta
            stats_ref[2:3, rows] = jnp.where(has_past, top + jnp.log2(total), -NEG_FILL)
            inverse_low = inverse.astype(BF16)
            probs = [weight * inverse_low for weight in weights]
            for keys, prob in zip(blocks, probs):
                dv_acc[keys, :] += matmul(prob, g_rows)
            for keys, prob, dprob in zip(blocks, probs, dprobs):
                dscore = prob * (dprob - delta).astype(BF16)
                dk_acc[keys, :] += matmul(dscore, q_rows)

        def nothing():
            inverse = 1.0 / own_sum
            stats_ref[0:1, rows] = inverse
            stats_ref[1:2, rows] = own_product * inverse
            stats_ref[2:3, rows] = jnp.full((1, ROW_BLOCK), -NEG_FILL, F32)

        past.by_units(chunk, nothing, branch)
        return carry

    lax.fori_loop(0, chunks, chunk_step, 0)
    stats_out.start()
    copies = [stats_out] + keep
    for slot in range(window):
        rows = slice(slot * past.tile_rows, (slot + 1) * past.tile_rows)
        shape = (past.n_owners, past.piece, width)
        terms_ref[0, slot] = (dk_acc[rows, :] * scale).astype(BF16).reshape(shape)
        terms_ref[1, slot] = dv_acc[rows, :].astype(BF16).reshape(shape)
        for part in range(2):
            copy = pltpu.make_async_copy(
                terms_ref.at[part, slot], terms_hbm.at[:, slot, part], terms_sem.at[part, slot]
            )
            copy.start()
            copies.append(copy)
    wait_all(copies)


def late_kernel(
    window,
    heads,
    q_hbm,
    g_hbm,
    stats_hbm,
    past_hbm,
    own_out_hbm,
    own_dq_hbm,
    summed_hbm,
    att_hbm,
    dq_hbm,
    q_ref,
    g_ref,
    stats_ref,
    win_ref,
    own_out_ref,
    own_dq_ref,
    att_ref,
    dq_ref,
    in_sem,
    past_sem,
    stats_sem,
    out_sem,
):
    past = Past(window, heads, past_hbm, win_ref)
    width = past.width
    scale = float(width) ** (-0.5)
    exponent_scale = scale * LOG2E
    chunks = q_ref.shape[0] // ROW_BLOCK
    pairs = (
        (q_hbm, q_ref, 0),
        (g_hbm, g_ref, 0),
        (own_out_hbm, own_out_ref, 1),
        (own_dq_hbm, own_dq_ref, 1),
    )
    out_pairs = ((att_ref, att_hbm, 0), (dq_ref, dq_hbm, 0))
    stats_in = pltpu.make_async_copy(stats_hbm.at[0:8], stats_ref, stats_sem.at[0])
    window_in = past.copies(0, past_sem) + past.copies(1, past_sem) + [stats_in]
    start_all(window_in)
    for chunk in range(chunks):
        start_all(chunk_copies(pairs, in_sem, chunk))
    wait_all(window_in)
    past.plan(stats_ref)

    def chunk_step(chunk, carry):
        rows = chunk_rows(chunk)
        wait_all(chunk_copies(pairs, in_sem, chunk))

        def branch(units):
            q_rows = q_ref[rows, :]
            g_rows = g_ref[rows, :]
            delta = stats_ref[1:2, rows]
            shift = stats_ref[2:3, rows]
            blocks, scores = past.scores(units, q_rows)
            out_turned = own_out_ref[:, rows].astype(F32)
            dq_turned = own_dq_ref[:, rows].astype(F32)
            for keys, score in zip(blocks, scores):
                prob = jnp.exp2(score * exponent_scale - shift).astype(BF16)
                out_turned += matmul_first(past.rows(1, keys), prob)
                dprob = matmul_last(past.rows(1, keys), g_rows)
                dscore = prob * (dprob - delta).astype(BF16)
                dq_turned += matmul_first(past.rows(0, keys), dscore)
            att_ref[rows, :] = out_turned.astype(BF16).T
            dq_ref[rows, :] = (dq_turned * scale).astype(BF16).T

        def nothing():
            att_ref[rows, :] = own_out_ref[:, rows].T
            dq_ref[rows, :] = (own_dq_ref[:, rows].astype(F32) * scale).astype(BF16).T

        past.by_units(chunk, nothing, branch)
        start_all(chunk_copies(out_pairs, out_sem, chunk))
        return carry

    lax.fori_loop(0, chunks, chunk_step, 0)
    for chunk in range(chunks):
        wait_all(chunk_copies(out_pairs, out_sem, chunk))


def own_grads_kernel(
    heads, q_ref, g_ref, stats_hbm, k_ref, v_ref, *refs
):
    tile_rows, width = k_ref.shape
    chunk_pos = ROW_BLOCK // heads
    chunks = q_ref.shape[0] // ROW_BLOCK
    weight_refs = refs[:chunks]
    out_ref, dq_ref, dkv_ref, stats_ref, stats_sem, dk_acc, dv_acc = refs[chunks:]
    scale = float(width) ** (-0.5)
    stats_in = pltpu.make_async_copy(stats_hbm.at[0:8], stats_ref, stats_sem.at[0])
    stats_in.start()
    dk_acc[...] = jnp.zeros_like(dk_acc)
    dv_acc[...] = jnp.zeros_like(dv_acc)
    stats_in.wait()

    for chunk, rows in enumerate(row_blocks(q_ref.shape[0])):
        rescale = stats_ref[0:1, rows]
        delta = stats_ref[1:2, rows]
        q_rows = q_ref[rows, :]
        g_rows = g_ref[rows, :]
        out_turned = jnp.zeros((width, ROW_BLOCK), F32)
        dq_turned = jnp.zeros((width, ROW_BLOCK), F32)
        for keys in key_blocks(0, (chunk + 1) * chunk_pos):
            prob = (weight_refs[chunk][keys, :].astype(F32) * rescale).astype(BF16)
            dprob = matmul_last(v_ref[keys, :], g_rows)
            dscore = prob * (dprob - delta).astype(BF16)
            dv_acc[keys, :] += matmul(prob, g_rows)
            dk_acc[keys, :] += matmul(dscore, q_rows)
            out_turned += matmul_first(v_ref[keys, :], prob)
            dq_turned += matmul_first(k_ref[keys, :], dscore)
        out_ref[:, rows] = out_turned.astype(BF16)
        dq_ref[:, rows] = dq_turned.astype(BF16)

    dkv_ref[0] = (dk_acc[...] * scale).astype(BF16)
    dkv_ref[1] = dv_acc[...].astype(BF16)


def holders(tile_of_ref, holder):
    n_ctx = tile_of_ref.shape[0]
    for ctx in range(n_ctx):
        holder[tile_of_ref[ctx]] = ctx


def route_kernel(window, place_ref, tile_of_ref, held_hbm, out_hbm, holder, sem):
    group, n_head = out_hbm.shape[:2]
    holders(tile_of_ref, holder)
    first = lax.div(place_ref[0], group) * group
    for member in range(group):
        for slot in range(window):
            tile = tile_of_ref[first + member] - (window - slot)
            source = holder[jnp.maximum(tile, 0)]
            for head in range(n_head):
                pltpu.make_async_copy(
                    held_hbm.at[source], out_hbm.at[member, head, slot], sem.at[member]
                ).start()
    for member in range(group):
        whole = out_hbm.at[member]
        pltpu.make_async_copy(whole, whole, sem.at[member]).wait()


def sum_kernel(window, group, place_ref, tile_of_ref, terms_ref, out_hbm, holder, summed, sem):
    n_ctx, n_head = out_hbm.shape[:2]
    holders(tile_of_ref, holder)
    first = lax.div(place_ref[0], group) * group

    for ctx in range(n_ctx):
        total = jnp.zeros(summed.shape[1:], F32)
        for slot in range(window):
            tile = tile_of_ref[ctx] + (window - slot)
            source = holder[jnp.minimum(tile, n_ctx - 1)] - first
            here = (tile < n_ctx) & (source >= 0) & (source < group)
            source = jnp.where(here, source, 0)
            part = terms_ref[source, 0, slot].astype(F32)
            for head in range(1, n_head):
                part = part + terms_ref[source, head, slot].astype(F32)
            total = total + jnp.where(here, part, 0.0)
        summed[ctx] = total.astype(BF16)
        for head in range(n_head):
            pltpu.make_async_copy(summed.at[ctx], out_hbm.at[ctx, head], sem.at[head]).start()
    for head in range(n_head):
        pltpu.make_async_copy(summed, out_hbm.at[:, head], sem.at[head]).wait()


def shape_of(shape, dtype):
    return jax.ShapeDtypeStruct(shape, dtype)


def call(body, name, specs, out_shape, scratch, flops, space=VMEM, limit=VMEM_LIMIT, aliases=()):
    return pl.pallas_call(
        body,
        in_specs=specs,
        out_specs=space if isinstance(space, list) else [space] * len(out_shape),
        out_shape=out_shape,
        scratch_shapes=scratch,
        compiler_params=pltpu.CompilerParams(vmem_limit_bytes=limit),
        cost_estimate=pl.CostEstimate(
            flops=flops, bytes_accessed=1 << 22, transcendentals=0
        ),
        input_output_aliases=dict(aliases),
        name=name,
    )


def stats_shape(row_total):
    return shape_of((STATS_SIZE // row_total, row_total), F32)


def past_call(window, heads, pieces_shape, row_total, work):
    n_owners, _, _, piece, width = pieces_shape
    past_rows = window * n_owners * piece
    chunks = row_total // ROW_BLOCK
    rows = pltpu.VMEM((row_total, width), BF16)
    stats = pltpu.VMEM((8, row_total), F32)
    win = pltpu.VMEM((2, window, n_owners, piece, width), BF16)
    acc = pltpu.VMEM((past_rows, width), F32)
    dma = pltpu.SemaphoreType.DMA
    return call(
        functools.partial(past_kernel, window, heads),
        "past",
        [HBM] * 3 + [ANY, HBM],
        (
            stats_shape(row_total),
            shape_of(pieces_shape, BF16),
            shape_of(pieces_shape, BF16),
        ),
        [
            rows,
            rows,
            stats,
            stats,
            win,
            win,
            acc,
            acc,
            dma((chunks, 2)),
            dma((2, window)),
            dma((2,)),
            dma((2, window)),
            dma((2, window)),
        ],
        4 * window * work,
        HBM,
        PAST_LIMIT,
        ((4, 2),),
    )


def late_call(window, heads, pieces_shape, row_total, work):
    n_owners, _, _, piece, width = pieces_shape
    chunks = row_total // ROW_BLOCK
    rows = pltpu.VMEM((row_total, width), BF16)
    columns = pltpu.VMEM((width, row_total), BF16)
    dma = pltpu.SemaphoreType.DMA
    return call(
        functools.partial(late_kernel, window, heads),
        "late",
        [HBM] * 7,
        (shape_of((row_total, width), BF16), shape_of((row_total, width), BF16)),
        [
            rows,
            rows,
            pltpu.VMEM((8, row_total), F32),
            pltpu.VMEM((2, window, n_owners, piece, width), BF16),
            columns,
            columns,
            rows,
            rows,
            dma((chunks, 4)),
            dma((2, window)),
            dma((1,)),
            dma((chunks, 2)),
        ],
        4 * window * work,
        HBM,
    )


def own_forward_call(heads, tile_rows, width, row_total, work):
    chunk_pos = ROW_BLOCK // heads
    ends = range(chunk_pos, tile_rows + 1, chunk_pos)
    return call(
        functools.partial(own_forward_kernel, heads),
        "own_forward",
        [SMEM] * 3 + [VMEM] * 4,
        (stats_shape(row_total),) + tuple(shape_of((end, ROW_BLOCK), BF16) for end in ends),
        [pltpu.VMEM((8, row_total), F32), pltpu.SemaphoreType.DMA((1,))],
        2 * work,
        [HBM] + [VMEM] * len(ends),
    )


def own_grads_call(heads, tile_rows, width, row_total, work):
    return call(
        functools.partial(own_grads_kernel, heads),
        "own_grads",
        [VMEM] * 2 + [HBM] + [VMEM] * (2 + row_total // ROW_BLOCK),
        (
            shape_of((width, row_total), BF16),
            shape_of((width, row_total), BF16),
            shape_of((2, tile_rows, width), BF16),
        ),
        [
            pltpu.VMEM((8, row_total), F32),
            pltpu.SemaphoreType.DMA((1,)),
            pltpu.VMEM((tile_rows, width), F32),
            pltpu.VMEM((tile_rows, width), F32),
        ],
        4 * work,
    )


def small_call(body, name, scalars, specs, out_shape, scratch):
    return pl.pallas_call(
        body,
        in_specs=[SMEM] * scalars + specs,
        out_specs=HBM,
        out_shape=out_shape,
        scratch_shapes=scratch,
        compiler_params=pltpu.CompilerParams(vmem_limit_bytes=SMALL_LIMIT),
        name=name,
    )


def on_device(queries, keys, values, grad_out, lengths, tile_of):
    tile_rows, heads, width = queries.shape
    n_ctx = lax.axis_size("ctx")
    n_head = lax.axis_size("head")
    group = n_ctx // 2
    n_owners = group * n_head
    piece = tile_rows // n_owners
    both = ("ctx", "head")
    halves = [list(range(n_owners)), list(range(n_owners, 2 * n_owners))]
    most_doc = n_ctx * tile_rows // 8
    window = -(-(most_doc - 1) // tile_rows)
    row_total = tile_rows * heads
    place = lax.axis_index("ctx").astype(jnp.int32).reshape(1)
    y = lax.axis_index("head")
    scalars = (place, lengths, tile_of)
    q_rows = queries.reshape(row_total, width)
    g_rows = grad_out.reshape(row_total, width)
    work = 2 * row_total * tile_rows * width
    fine = piece % 16 == 0

    shape = (2, group, 1, piece, width)
    mine = [
        lax.dynamic_index_in_dim(tile.reshape(group, n_head, piece, width), y, 1)
        for tile in (keys, values)
    ]
    mine = jnp.concatenate([jnp.broadcast_to(part[None], shape) for part in mine], axis=2)
    held = lax.all_to_all(
        mine.reshape(n_ctx, 2, piece, width), "ctx", 0, 0, tiled=True
    )
    packed = small_call(
        functools.partial(route_kernel, window),
        "route",
        2,
        [ANY],
        shape_of((group, n_head, window, 2, piece, width), BF16),
        [pltpu.SMEM((n_ctx,), jnp.int32), pltpu.SemaphoreType.DMA((group,))],
    )(place, tile_of, held)
    past = lax.all_to_all(
        packed.reshape(n_owners, window, 2, piece, width),
        both,
        0,
        0,
        tiled=True,
        axis_index_groups=halves,
    )
    pieces_shape = (n_owners, window, 2, piece, width)
    if not fine:
        pieces_shape = (1, window, 2, tile_rows, width)
        past = past.transpose(1, 2, 0, 3, 4).reshape(pieces_shape)

    own_stats, *own_weights = own_forward_call(heads, tile_rows, width, row_total, work)(
        *scalars, q_rows, g_rows, keys, values
    )
    stats, terms, kept = past_call(window, heads, pieces_shape, row_total, work)(
        q_rows, g_rows, own_stats, past, packed.reshape(pieces_shape)
    )
    own_out, own_dq, own_grads = own_grads_call(heads, tile_rows, width, row_total, work)(
        q_rows, g_rows, stats, keys, values, *own_weights
    )

    if not fine:
        terms = terms.reshape(window, 2, n_owners, piece, width).transpose(2, 0, 1, 3, 4)
    terms = lax.all_to_all(terms, both, 0, 0, tiled=True, axis_index_groups=halves)
    terms, own_grads = lax.optimization_barrier((terms, own_grads))
    summed = small_call(
        functools.partial(sum_kernel, window, group),
        "sum_terms",
        2,
        [VMEM],
        shape_of((n_ctx, n_head, 2, piece, width), BF16),
        [
            pltpu.SMEM((n_ctx,), jnp.int32),
            pltpu.VMEM((n_ctx, 2, piece, width), BF16),
            pltpu.SemaphoreType.DMA((n_head,)),
        ],
    )(place, tile_of, terms.reshape(group, n_head, window, 2, piece, width))
    summed = summed.reshape(n_ctx * n_head, 2, piece, width)
    far = lax.all_to_all(summed, both, 0, 0, tiled=True)
    attended, query_grad = late_call(window, heads, pieces_shape, row_total, work)(
        q_rows, g_rows, stats, kept, own_out, own_dq, summed
    )

    if n_head == 2:
        peer = lax.ppermute(own_grads, "head", [(0, 1), (1, 0)])
        peer, far, attended = lax.optimization_barrier((peer, far, attended))
        near = own_grads.astype(F32) + peer.astype(F32)
    else:
        near = lax.psum(own_grads.astype(F32), "head")
    far = far.reshape(2, n_owners, 2, piece, width).astype(F32)
    far = far[0] + far[1]
    far_keys, far_values = (far[:, part].reshape(tile_rows, width) for part in range(2))
    return (
        attended.reshape(tile_rows, heads, width),
        query_grad.reshape(tile_rows, heads, width),
        near[0] + far_keys,
        near[1] + far_values,
    )


def solution(mesh):
    return jax.shard_map(
        on_device,
        mesh=mesh,
        in_specs=(
            P("ctx", "head", None),
            P("ctx", None),
            P("ctx", None),
            P("ctx", "head", None),
            P(),
            P(),
        ),
        out_specs=(P("ctx", "head", None), P("ctx", "head", None), P("ctx", None), P("ctx", None)),
        check_vma=False,
    )
```
